32 devices in a mesh: req: 8 (over z, x), mlp: 4 (over y, core).
Axes of the slice: x: 2, y: 2, z: 4, core: 2. Of those that a mesh axis runs over, the one named last changes fastest.
Arguments:
- residual_in: bfloat16 [8192, 1664], P('req'), may hold values from -6 to 6
- lengths: int32 [256], P(('req', 'mlp')), may hold values from 0 to 64, as said below
- owners: int32 [256], P(('req', 'mlp')), may hold values from 0 to 7, as said below
- merge_dest: int32 [8192], P('req'), may hold values from 0 to 255, as said below
- segment_ids: int32 [8192], P('req'), may hold values from 0 to 3, as said below
- norm2_gain: float32 [1664], replicated, may hold values from 0.5 to 1.5
- norm2_bias: float32 [1664], replicated, may hold values from -3 to 3
- up_weight: bfloat16 [4096, 1664], P('mlp'), may hold values from -0.15625 to 0.15625
- up_bias: float32 [4096], P('mlp'), may hold values from -3 to 3
- down_weight: bfloat16 [4096, 1664], P('mlp'), may hold values from -0.09375 to 0.09375
- down_bias: float32 [1664], replicated, may hold values from -3 to 3
- proj_weight: bfloat16 [6656, 1664], P('mlp'), may hold values from -0.078125 to 0.078125
- norm3_gain: float32 [1664], replicated, may hold values from 0.5 to 1.5
- norm3_bias: float32 [1664], replicated, may hold values from -3 to 3
- next_weight: bfloat16 [1664, 3, 1664], P('req'), may hold values from -0.15625 to 0.15625
Outputs:
- merged_out: bfloat16 [4096, 1664], P(('req', 'mlp'))
- next_mixed: bfloat16 [4096, 1664], P(('req', 'mlp'))
The draws below stay inside these ranges and needn't reach their ends.
Inputs may be any that keep to these rules, and one draw needn't show every extreme that they name: The 8 pieces of each block of 256 tokens (one device, req-major order) have lengths that are multiples of 4 and sum to 256; in every block one piece has exactly 64 tokens. The owners of the 8 pieces of one block are a permutation of 0 to 7; for each index of mlp, one piece of 64 tokens of each block of that index goes to one owner shared by all blocks of that index. `merge_dest`: within each device block a permutation of 0 to 255 that maps the tokens of each piece onto that piece's own positions. `segment_ids`: the four tokens of a block whose merge_dest values have the same quotient by 4 carry one segment id.
All inputs are finite; a program needn't handle non-finite values.
Results may differ from the reference program's by a relative error of at most 0.023.
Values may be sent and summed in bfloat16 or wider, within the bound.
A program may use at most 128 MiB of HBM per device.

```python
import math
import jax
import jax.numpy as jnp
from jax import lax

D = 1664
HEADS = 16
HEAD_DIM = 104
FF = 4096
TOK_DEV = 256
SEGS = 4
SLOTS = 16
TOKENS = 8192
N_REQ = 8
N_MLP = 4
DEVICES = 32


def shuffle_rows(key_base, count, length):

    def one_row(row_key):
        return jax.random.permutation(row_key, length)
    return jax.vmap(one_row)(jax.random.split(key_base, count))


def request_layout(key):
    base_key = jax.random.fold_in(key, 4321)
    key_fill, key_order, key_merge, key_owner, key_mark, key_full = jax.random.split(base_key, 6)
    unit_count = TOK_DEV // 4
    slot_count = TOK_DEV // (2 * N_REQ)
    cell_count = (N_REQ - 1) * slot_count
    taken = unit_count - slot_count
    cell_ranks = shuffle_rows(key_fill, DEVICES, cell_count)
    chosen = (cell_ranks < taken).astype(jnp.int32).reshape(DEVICES, N_REQ - 1, slot_count)
    bins = jnp.concatenate([jnp.full((DEVICES, 1), slot_count, jnp.int32), jnp.sum(chosen, axis=2).astype(jnp.int32)], axis=1)
    piece_order = shuffle_rows(key_order, DEVICES, N_REQ).astype(jnp.int32)
    units = jnp.take_along_axis(bins, piece_order, axis=1)
    lengths = 4 * units
    piece_ids = jnp.arange(N_REQ, dtype=jnp.int32)
    full_index = jnp.sum(piece_ids[None, :] * (piece_order == 0).astype(jnp.int32), axis=1)
    starts = jnp.cumsum(lengths, axis=1) - lengths
    positions = jnp.arange(TOK_DEV, dtype=jnp.int32)
    piece_of = jnp.sum((positions[None, :, None] >= starts[:, None, :]).astype(jnp.int32), axis=2) - 1
    shuffle = shuffle_rows(key_merge, DEVICES, TOK_DEV).astype(jnp.int32)
    token_order = jnp.argsort(piece_of * TOK_DEV + shuffle, axis=1)
    merge_places = jnp.argsort(token_order, axis=1).astype(jnp.int32)
    row_marks = jax.random.randint(key_mark, (DEVICES, unit_count), 0, SEGS).astype(jnp.int32)
    token_marks = jnp.take_along_axis(row_marks, merge_places // 4, axis=1)
    permuted = shuffle_rows(key_owner, DEVICES, N_REQ).astype(jnp.int32)
    lane_owner = jax.random.randint(key_full, (N_MLP,), 0, N_REQ).astype(jnp.int32)
    device_lane = jnp.arange(DEVICES, dtype=jnp.int32) % N_MLP
    wanted = jnp.take(lane_owner, device_lane)
    wanted_at = jnp.sum(piece_ids[None, :] * (permuted == wanted[:, None]).astype(jnp.int32), axis=1)
    value_at_full = jnp.sum(permuted * (piece_ids[None, :] == full_index[:, None]).astype(jnp.int32), axis=1)
    owner_rows = jnp.where(piece_ids[None, :] == full_index[:, None], wanted[:, None], jnp.where(piece_ids[None, :] == wanted_at[:, None], value_at_full[:, None], permuted))
    return (lengths.astype(jnp.int32), owner_rows.astype(jnp.int32), merge_places, token_marks.astype(jnp.int32))


def draw_lengths(key, part):
    return request_layout(key)[0].reshape(DEVICES * N_REQ)


def draw_owners(key, part):
    return request_layout(key)[1].reshape(DEVICES * N_REQ)


def draw_merge_dest(key, part):
    return request_layout(key)[2].reshape(DEVICES * TOK_DEV)


def draw_segment_ids(key, part):
    return request_layout(key)[3].reshape(DEVICES * TOK_DEV)


def block_scale(stream_key, extent, cuts, least, high):
    def one(position, blocks):
        draws = jax.random.uniform(jax.random.fold_in(jax.random.fold_in(stream_key, 6), position), (blocks,), jnp.float32, least / len(cuts), high / len(cuts))
        return jnp.repeat(jnp.exp(draws), extent[position] // blocks).reshape((-1,) + (1,) * (len(extent) - position - 1))

    loudness = one(*cuts[0])
    for cut in cuts[1:]:
        loudness = loudness * one(*cut)
    return loudness


def gaussian(own_key, shape, deviation, reach, cuts=(), kind=jnp.bfloat16):
    drawn = deviation * jax.random.normal(own_key, shape, jnp.float32)
    if cuts:
        drawn = drawn * block_scale(own_key, shape, cuts, -0.22, 0.18)
    return jnp.clip(drawn, -reach, reach).astype(kind)


def setup_inputs(seed: int = 0) -> dict:
    key_of = jax.random.split(jax.random.key(seed), 16)
    residual_in = gaussian(key_of[0], (TOKENS, D), 1.0, 6.0, ((0, 8),))
    lengths = draw_lengths(jax.random.fold_in(key_of[15], 71), 0)
    owners = draw_owners(jax.random.fold_in(key_of[15], 71), 0)
    merge_dest = draw_merge_dest(jax.random.fold_in(key_of[15], 71), 0)
    segment_ids = draw_segment_ids(jax.random.fold_in(key_of[15], 71), 0)
    norm2_gain = jnp.clip(1.0 + 0.1 * jax.random.normal(key_of[5], (D,), jnp.float32), 0.5, 1.5)
    norm2_bias = gaussian(key_of[6], (D,), 0.5, 3.0, (), jnp.float32)
    up_weight = gaussian(key_of[7], (FF, D), D ** -0.5, 0.15625, ((0, 4),))
    up_bias = gaussian(key_of[8], (FF,), 0.5, 3.0, ((0, 4),), jnp.float32)
    down_weight = gaussian(key_of[9], (FF, D), FF ** -0.5, 0.09375, ((0, 4),))
    down_bias = gaussian(key_of[10], (D,), 0.5, 3.0, (), jnp.float32)
    proj_weight = gaussian(key_of[11], (4 * D, D), (4 * D) ** -0.5, 0.078125, ((0, 4),))
    norm3_gain = jnp.clip(1.0 + 0.1 * jax.random.normal(key_of[12], (D,), jnp.float32), 0.5, 1.5)
    norm3_bias = gaussian(key_of[13], (D,), 0.5, 3.0, (), jnp.float32)
    next_weight = gaussian(key_of[14], (D, 3, D), D ** -0.5, 0.15625, ((0, 8),))
    return {"residual_in": residual_in, "lengths": lengths, "owners": owners, "merge_dest": merge_dest, "segment_ids": segment_ids, "norm2_gain": norm2_gain, "norm2_bias": norm2_bias, "up_weight": up_weight, "up_bias": up_bias, "down_weight": down_weight, "down_bias": down_bias, "proj_weight": proj_weight, "norm3_gain": norm3_gain, "norm3_bias": norm3_bias, "next_weight": next_weight}


EPSILON = 1e-06

def layer_norm(rows, gain, bias):
    values = rows.astype(jnp.float32)
    mean_value = lax.optimization_barrier(jnp.mean(values, axis=-1, keepdims=True))
    centred = values - mean_value
    spread = lax.optimization_barrier(jnp.mean(centred * centred, axis=-1, keepdims=True))
    return centred * lax.rsqrt(spread + EPSILON) * gain + bias

def block_attention(pair):
    heads_block, tag_block = pair
    queries = heads_block[:, 0].astype(jnp.float32)
    key_rows = heads_block[:, 1].astype(jnp.float32)
    value_rows = heads_block[:, 2].astype(jnp.float32)
    score_scale = 1.0 / math.sqrt(heads_block.shape[-1])
    scores = jnp.einsum('qhe,khe->hqk', queries, key_rows) * score_scale
    slot_total = heads_block.shape[0]
    itself = lax.broadcasted_iota(jnp.int32, (slot_total, slot_total), 0) == lax.broadcasted_iota(jnp.int32, (slot_total, slot_total), 1)
    live_slots = tag_block >= 0
    same_request = tag_block[:, None] == tag_block[None, :]
    allowed = same_request & live_slots[None, :] | itself
    weights = jnp.where(allowed[None], jnp.exp(scores), 0.0)
    probs = (weights / lax.optimization_barrier(jnp.sum(weights, axis=-1, keepdims=True))).astype(jnp.bfloat16)
    mixed_out = jnp.einsum('hqk,khe->qhe', probs.astype(jnp.float32), value_rows)
    mixed_out = jnp.where(live_slots[:, None, None], mixed_out, 0.0)
    return mixed_out.astype(jnp.bfloat16)

def reference(residual_in, lengths, owners, merge_dest, segment_ids, norm2_gain, norm2_bias, up_weight, up_bias, down_weight, down_bias, proj_weight, norm3_gain, norm3_bias, next_weight):
    group_rows = TOK_DEV * N_MLP

    def feed_group(rows):
        normed = layer_norm(rows, norm2_gain, norm2_bias).astype(jnp.bfloat16)
        upward = lax.dot_general(normed, up_weight, (((1,), (1,)), ((), ())), preferred_element_type=jnp.float32)
        hidden = jax.nn.gelu(upward + up_bias, approximate=False).astype(jnp.bfloat16)
        feed_out = jnp.dot(hidden, down_weight, preferred_element_type=jnp.float32)
        return (rows.astype(jnp.float32) + feed_out + down_bias).astype(jnp.bfloat16)
    layer_out = lax.map(feed_group, residual_in.reshape(N_REQ, group_rows, D))
    blocks = layer_out.reshape(DEVICES, TOK_DEV, D)
    places = merge_dest.reshape(DEVICES, TOK_DEV)
    marks = segment_ids.reshape(DEVICES, TOK_DEV)

    def merge_block(triple):
        rows, dest_block, mark_block = triple
        source = jnp.zeros((TOK_DEV,), jnp.int32).at[dest_block].set(jnp.arange(TOK_DEV, dtype=jnp.int32))
        merged_rows = jnp.take(rows, source, axis=0).reshape(TOK_DEV // 4, 4 * D)
        row_segment = jnp.take(mark_block, source.reshape(TOK_DEV // 4, 4)[:, 0], axis=0)
        return (merged_rows, row_segment)
    merged, row_segment = lax.map(merge_block, (blocks, places, marks))
    merged = merged.reshape(DEVICES * (TOK_DEV // 4), 4 * D)
    projected = jnp.dot(merged, proj_weight, preferred_element_type=jnp.float32).astype(jnp.bfloat16)
    per_device = TOK_DEV // 4
    counts = (lengths // 4).reshape(DEVICES, N_REQ)
    starts = jnp.cumsum(counts, axis=1) - counts
    index = jnp.arange(per_device, dtype=jnp.int32)
    inside = ((index[None, :, None] >= starts[:, None, :]) & (index[None, :, None] < (starts + counts)[:, None, :])).astype(jnp.int32)
    piece_owner = owners.reshape(DEVICES, N_REQ)
    owner_of = lax.optimization_barrier(jnp.sum(inside * piece_owner[:, None, :], axis=2))
    rank = index[None, :] - lax.optimization_barrier(jnp.sum(inside * starts[:, None, :], axis=2))
    device = jnp.arange(DEVICES, dtype=jnp.int32)
    sender = device // N_MLP
    lane_of = device % N_MLP
    recv_rows = N_REQ * SLOTS
    target = (owner_of * N_MLP + lane_of[:, None]) * recv_rows + sender[:, None] * SLOTS + rank
    merged_out = jnp.zeros((DEVICES * recv_rows, D), jnp.bfloat16).at[target.reshape(-1)].set(projected)
    slot_segment = jnp.full((DEVICES * recv_rows,), -1, jnp.int32).at[target.reshape(-1)].set(row_segment.reshape(-1))
    normed3 = layer_norm(merged_out, norm3_gain, norm3_bias).astype(jnp.bfloat16)
    heads_in = jnp.dot(normed3, next_weight.reshape(D, 3 * D), preferred_element_type=jnp.float32).astype(jnp.bfloat16)
    heads_in = heads_in.reshape(DEVICES, recv_rows, 3, HEADS, HEAD_DIM)
    next_mixed = lax.map(block_attention, (heads_in, slot_segment.reshape(DEVICES, recv_rows)))
    return (merged_out, next_mixed.reshape(DEVICES * recv_rows, D))
```

```python
import math

import jax
import jax.numpy as jnp
from jax import lax
from jax.sharding import PartitionSpec as P

HEAD_DIM = 104
TAG_PAD = 128
EPSILON = 1e-06


def layer_norm(rows, gain, bias):
    values = rows.astype(jnp.float32)
    mean_value = jnp.mean(values, axis=-1, keepdims=True)
    centred = values - mean_value
    spread = jnp.mean(centred * centred, axis=-1, keepdims=True)
    return centred * lax.rsqrt(spread + EPSILON) * gain + bias


def block_attention(heads_in, slot_tags):
    queries = heads_in[:, :, 0]
    key_rows = heads_in[:, :, 1]
    value_rows = heads_in[:, :, 2]
    score_scale = 1.0 / math.sqrt(heads_in.shape[-1])
    scores = (
        jnp.einsum("bqhe,bkhe->bhqk", queries, key_rows, preferred_element_type=jnp.float32)
        * score_scale
    )
    slot_total = heads_in.shape[1]
    itself = lax.broadcasted_iota(jnp.int32, (slot_total, slot_total), 0) == lax.broadcasted_iota(
        jnp.int32, (slot_total, slot_total), 1
    )
    live_slots = slot_tags >= 0
    same_request = slot_tags[:, :, None] == slot_tags[:, None, :]
    allowed = same_request & live_slots[:, None, :] | itself[None]
    weights = jnp.where(allowed[:, None], jnp.exp(scores), 0.0)
    probs = (weights / jnp.sum(weights, axis=-1, keepdims=True)).astype(jnp.bfloat16)
    mixed_out = jnp.einsum("bhqk,bkhe->bqhe", probs, value_rows, preferred_element_type=jnp.float32)
    mixed_out = jnp.where(live_slots[:, :, None, None], mixed_out, 0.0)
    return mixed_out.astype(jnp.bfloat16)


def body(
    residual_in,
    lengths,
    owners,
    merge_dest,
    segment_ids,
    norm2_gain,
    norm2_bias,
    up_weight,
    up_bias,
    down_weight,
    down_bias,
    proj_weight,
    norm3_gain,
    norm3_bias,
    next_weight,
):
    group_rows, model_width = residual_in.shape
    lane_count = lax.axis_size("mlp")
    sender_count = lax.axis_size("req")
    lane_index = lax.axis_index("mlp")
    own_rows = group_rows // lane_count
    merged_rows = own_rows // 4
    slot_count = 2 * merged_rows // sender_count
    part_width = model_width // lane_count
    own_columns = lax.dynamic_slice_in_dim(
        next_weight.transpose(1, 0, 2), lane_index * part_width, part_width, 2
    )
    piece = lax.all_gather(own_columns, "req", axis=1, tiled=True)
    places = merge_dest.reshape(lane_count, own_rows)
    wanted = (
        4 * lax.broadcasted_iota(jnp.int32, (4, merged_rows), 1)
        + lax.broadcasted_iota(jnp.int32, (4, merged_rows), 0)
    )
    hits = wanted[:, None, :, None] == places[None, :, None, :]
    ordered = jnp.einsum(
        "qbit,btd->qbid",
        hits.astype(jnp.bfloat16),
        residual_in.reshape(lane_count, own_rows, model_width),
        preferred_element_type=jnp.float32,
    ).astype(jnp.bfloat16).reshape(group_rows, model_width)
    normed = layer_norm(ordered, norm2_gain, norm2_bias).astype(jnp.bfloat16)
    upward = lax.dot_general(
        normed, up_weight, (((1,), (1,)), ((), ())), preferred_element_type=jnp.float32
    )
    hidden = jax.nn.gelu(upward + up_bias, approximate=False).astype(jnp.bfloat16)
    partial_sums = jnp.dot(hidden, down_weight, preferred_element_type=jnp.float32)
    feed_out = lax.psum_scatter(
        partial_sums.astype(jnp.bfloat16), "mlp", scatter_dimension=0, tiled=True
    ).astype(jnp.float32)
    own_quarter = lax.dynamic_slice_in_dim(ordered, lane_index * own_rows, own_rows, 0)
    quarter = (own_quarter.astype(jnp.float32) + feed_out + down_bias).astype(jnp.bfloat16)
    projected = lax.psum_scatter(
        jnp.dot(quarter, proj_weight, preferred_element_type=jnp.float32).astype(jnp.bfloat16),
        "mlp",
        scatter_dimension=0,
        tiled=True,
    )
    own_places = lax.dynamic_index_in_dim(places, lane_index, 0, False)
    own_marks = lax.dynamic_index_in_dim(
        segment_ids.reshape(lane_count, own_rows), lane_index, 0, False
    )
    row_segment = jnp.sum(
        (wanted[0][:, None] == own_places[None, :]).astype(jnp.int32) * own_marks[None, :], axis=1
    )
    counts = lengths // 4
    starts = jnp.cumsum(counts) - counts
    index = lax.broadcasted_iota(jnp.int32, (merged_rows, 1), 0)
    inside = ((index >= starts[None, :]) & (index < (starts + counts)[None, :])).astype(jnp.int32)
    owner_of = jnp.sum(inside * owners[None, :], axis=1)
    rank = index[:, 0] - jnp.sum(inside * starts[None, :], axis=1)
    target = owner_of * slot_count + rank
    slot_ids = lax.broadcasted_iota(jnp.int32, (sender_count * slot_count, 1), 0)
    route_hits = slot_ids == target[None, :]
    outgoing = jnp.dot(
        route_hits.astype(jnp.bfloat16), projected, preferred_element_type=jnp.float32
    ).astype(jnp.bfloat16)
    sent_tags = jnp.sum(route_hits.astype(jnp.int32) * (row_segment + 1)[None, :], axis=1) - 1
    tag_columns = jnp.broadcast_to(
        sent_tags.astype(jnp.bfloat16)[:, None], (sent_tags.shape[0], TAG_PAD)
    )
    arrived = lax.all_to_all(
        jnp.concatenate([outgoing, tag_columns], axis=1),
        "req", split_axis=0, concat_axis=0, tiled=True,
    )
    received = arrived[:, :model_width]
    normed3 = layer_norm(received, norm3_gain, norm3_bias).astype(jnp.bfloat16)
    recv_rows = received.shape[0]
    everyone = lax.all_gather(
        jnp.concatenate([normed3, arrived[:, model_width:]], axis=1), "mlp", axis=0, tiled=True
    )
    tags = everyone[:, model_width].astype(jnp.int32).reshape(lane_count, recv_rows)
    heads_in = jnp.einsum(
        "rd,sde->rse", everyone[:, :model_width], piece, preferred_element_type=jnp.float32
    )
    heads_in = heads_in.astype(jnp.bfloat16).reshape(lane_count, recv_rows, 3, -1, HEAD_DIM)
    mixed = block_attention(heads_in, tags).reshape(lane_count * recv_rows, part_width)
    next_mixed = lax.all_to_all(mixed, "mlp", split_axis=0, concat_axis=1, tiled=True)
    return (received, next_mixed)


def solution(mesh):
    return jax.shard_map(
        body,
        mesh=mesh,
        in_specs=(
            P("req", None),
            P(("req", "mlp")),
            P(("req", "mlp")),
            P("req"),
            P("req"),
            P(),
            P(),
            P("mlp", None),
            P("mlp"),
            P("mlp", None),
            P(),
            P("mlp", None),
            P(),
            P(),
            P("req", None, None),
        ),
        out_specs=(P(("req", "mlp"), None), P(("req", "mlp"), None)),
        check_vma=False,
    )
```

```python
import functools
import math

import jax
import jax.numpy as jnp
from jax import lax
from jax.experimental import pallas as pl
from jax.experimental.pallas import tpu as pltpu
from jax.sharding import PartitionSpec as P

HEAD_DIM = 104
TAG_PAD = 128
EPSILON = 1e-06


VMEM_BYTES = 56 * 2**20
MESH = pl.DeviceIdType.MESH


def front_kernel(
    sizes,
    places_ref,
    marks_ref,
    len_row_ref,
    len_col_ref,
    own_col_ref,
    gain2_ref,
    bias2_ref,
    up_bias_ref,
    down_bias_ref,
    gain3_ref,
    bias3_ref,
    residual_hbm,
    up_hbm,
    down_hbm,
    proj_hbm,
    merged_ref,
    everyone_ref,
    residual_ref,
    up_ref,
    down_ref,
    proj_ref,
    xq_ref,
    hidden_ref,
    acc_ref,
    core_out_ref,
    core_in_ref,
    y_out_ref,
    y_in_ref,
    share_ref,
    share_in_ref,
    out_ref,
    in_ref,
    load_sem,
    core_send,
    core_recv,
    y_send,
    y_recv,
    share_send,
    share_recv,
    req_send,
    req_recv,
    all_send,
    all_recv,
):
    senders, slots, pad = sizes
    lanes = 4
    m = lax.axis_index("mlp")
    r = lax.axis_index("req")
    core_peer = m + 1 - 2 * (m % 2)
    y_peer = (m + 2) % lanes
    own_rows = places_ref.shape[-1]
    merged = own_rows // 4
    width = residual_ref.shape[1]
    wide = out_ref.shape[1]

    loads = [
        pltpu.make_async_copy(a, b, load_sem.at[i])
        for i, (a, b) in enumerate(
            ((residual_hbm, residual_ref), (up_hbm, up_ref), (down_hbm, down_ref), (proj_hbm, proj_ref))
        )
    ]
    for load in loads:
        load.start()

    barrier = pltpu.get_barrier_semaphore()
    for k in range(1, lanes):
        pl.semaphore_signal(barrier, inc=1, device_id={"mlp": (m + k) % lanes}, device_id_type=MESH)

    def greet(k, c):
        pl.semaphore_signal(barrier, inc=1, device_id={"req": (r + k) % senders}, device_id_type=MESH)
        return c

    lax.fori_loop(1, senders, greet, 0)
    pl.semaphore_wait(barrier, lanes - 1 + senders - 1)

    def norm(values, gain, bias):
        mean_value = jnp.mean(values, axis=-1, keepdims=True)
        centred = values - mean_value
        spread = jnp.mean(centred * centred, axis=-1, keepdims=True)
        return centred * lax.rsqrt(spread + EPSILON) * gain + bias

    def core_copy(i):
        return pltpu.make_async_remote_copy(
            src_ref=core_out_ref.at[i], dst_ref=core_in_ref.at[i],
            send_sem=core_send.at[i], recv_sem=core_recv.at[i],
            device_id={"mlp": core_peer}, device_id_type=MESH,
        )

    y_copy = pltpu.make_async_remote_copy(
        src_ref=y_out_ref, dst_ref=y_in_ref, send_sem=y_send, recv_sem=y_recv,
        device_id={"mlp": y_peer}, device_id_type=MESH,
    )

    loads[0].wait()

    def quadrant_step(step, c):
        first = 1 - step // 2
        second = 1 - step % 2
        q = (1 - second) * m + second * core_peer
        q = (1 - first) * q + first * ((q + 2) % lanes)
        want = 4 * lax.broadcasted_iota(jnp.int32, (merged, own_rows), 0) + q
        for b in range(lanes):
            hits = (want == places_ref[b]).astype(jnp.float32).astype(jnp.bfloat16)
            xq_ref[b * merged : (b + 1) * merged, :] = jnp.dot(
                hits,
                residual_ref[b * own_rows : (b + 1) * own_rows, :],
                preferred_element_type=jnp.float32,
            )
        normed = norm(xq_ref[...], gain2_ref[...], bias2_ref[...]).astype(jnp.bfloat16)

        @pl.when(step == 0)
        def _():
            loads[1].wait()

        hidden_total = up_ref.shape[0]
        for j in range(0, hidden_total, 256):
            upward = lax.dot_general(
                normed, up_ref[j : j + 256, :], (((1,), (1,)), ((), ())),
                preferred_element_type=jnp.float32,
            ) + up_bias_ref[:, j : j + 256]
            hidden_ref[:, j : j + 256] = (
                0.5 * upward * (1.0 + lax.erf(upward * math.sqrt(0.5)))
            ).astype(jnp.bfloat16)

        @pl.when(step == 0)
        def _():
            loads[2].wait()

        acc_ref[...] = jnp.dot(hidden_ref[...], down_ref[...], preferred_element_type=jnp.float32)

        @pl.when(step == 0)
        def _():
            core_out_ref[0] = acc_ref[...].astype(jnp.bfloat16)
            core_copy(0).start()

        @pl.when(step == 1)
        def _():
            core_copy(0).wait_recv()
            y_out_ref[...] = (acc_ref[...] + core_in_ref[0].astype(jnp.float32)).astype(jnp.bfloat16)
            y_copy.start()

        @pl.when(step == 2)
        def _():
            core_out_ref[1] = acc_ref[...].astype(jnp.bfloat16)
            core_copy(1).start()

        return c

    lax.fori_loop(0, lanes, quadrant_step, 0)
    counts_row = len_row_ref[...] // 4
    counts_col = len_col_ref[...] // 4
    before = (
        lax.broadcasted_iota(jnp.int32, (senders, senders), 1)
        < lax.broadcasted_iota(jnp.int32, (senders, senders), 0)
    )
    starts = jnp.sum(jnp.where(before, counts_row, 0), axis=1, keepdims=True)
    index = lax.broadcasted_iota(jnp.int32, (senders, merged), 1)
    inside = (index >= starts) & (index < starts + counts_col)
    owner_of = jnp.sum(jnp.where(inside, own_col_ref[...], 0), axis=0, keepdims=True)
    begun = jnp.sum(jnp.where(inside, starts, 0), axis=0, keepdims=True)
    target = owner_of * pad + index[0:1, :] - begun
    route = (
        lax.broadcasted_iota(jnp.int32, (senders * pad, merged), 0) == target
    ).astype(jnp.float32).astype(jnp.bfloat16)
    first_hits = 4 * lax.broadcasted_iota(jnp.int32, (merged, own_rows), 0) == places_ref[m]
    row_tag = 1 + jnp.sum(jnp.where(first_hits, marks_ref[m], 0), axis=1, keepdims=True)
    tag_columns = jnp.broadcast_to(row_tag.astype(jnp.float32), (merged, wide - width))

    core_copy(1).wait_recv()
    y_copy.wait_recv()
    layer_out = (
        xq_ref[...] + (acc_ref[...] + core_in_ref[1].astype(jnp.float32) + y_in_ref[...].astype(jnp.float32))
        + down_bias_ref[...]
    ).astype(jnp.bfloat16)
    loads[3].wait()
    acc_ref[...] = jnp.dot(layer_out, proj_ref[...], preferred_element_type=jnp.float32)
    for b in range(lanes):
        share_ref[b] = acc_ref[b * merged : (b + 1) * merged, :].astype(jnp.bfloat16)
    shares = [
        pltpu.make_async_remote_copy(
            src_ref=share_ref.at[(m + k) % lanes], dst_ref=share_in_ref.at[k - 1],
            send_sem=share_send.at[k - 1], recv_sem=share_recv.at[k - 1],
            device_id={"mlp": (m + k) % lanes}, device_id_type=MESH,
        )
        for k in range(1, lanes)
    ]
    for share in shares:
        share.start()
    for share in shares:
        share.wait_recv()
    total = share_ref[m].astype(jnp.float32)
    for k in range(1, lanes):
        total = total + share_in_ref[k - 1].astype(jnp.float32)
    extended = jnp.concatenate([total, tag_columns], axis=1).astype(jnp.bfloat16)
    out_ref[...] = jnp.dot(route, extended, preferred_element_type=jnp.float32).astype(jnp.bfloat16)

    def req_copy(k):
        to = (r + k) % senders
        return pltpu.make_async_remote_copy(
            src_ref=out_ref.at[pl.ds(pl.multiple_of(to * pad, 16), pad)],
            dst_ref=in_ref.at[pl.ds(pl.multiple_of(r * pad, 16), pad)],
            send_sem=req_send.at[k - 1], recv_sem=req_recv.at[k - 1],
            device_id={"req": to}, device_id_type=MESH,
        )

    def start_req(k, c):
        req_copy(k).start()
        return c

    lax.fori_loop(1, senders, start_req, 0)
    own = pl.ds(pl.multiple_of(r * pad, 16), pad)
    in_ref[own, :] = out_ref[own, :]
    def wait_req(k, c):
        req_copy(k).wait_recv()
        return c

    lax.fori_loop(1, senders, wait_req, 0)
    arrived = in_ref[...]
    if pad != slots:
        row = lax.broadcasted_iota(jnp.int32, (senders * slots, senders * pad), 0)
        column = lax.broadcasted_iota(jnp.int32, (senders * slots, senders * pad), 1)
        pick = (row // slots * pad + row % slots == column).astype(jnp.float32).astype(jnp.bfloat16)
        arrived = jnp.dot(pick, arrived, preferred_element_type=jnp.float32).astype(jnp.bfloat16)
    received = arrived[:, :width]
    merged_ref[...] = received
    everyone_ref[m, :, width:] = arrived[:, width:]
    everyone_ref[m, :, :width] = norm(
        received.astype(jnp.float32), gain3_ref[...], bias3_ref[...]
    ).astype(jnp.bfloat16)

    def row_copy(slot, block, peer):
        return pltpu.make_async_remote_copy(
            src_ref=everyone_ref.at[block], dst_ref=everyone_ref.at[block],
            send_sem=all_send.at[slot], recv_sem=all_recv.at[slot],
            device_id={"mlp": peer}, device_id_type=MESH,
        )

    row_y = row_copy(0, m, y_peer)
    row_core = row_copy(1, m, core_peer)
    row_y.start()
    row_core.start()
    row_y.wait_recv()
    row_far = row_copy(2, y_peer, core_peer)
    row_far.start()
    row_core.wait_recv()
    row_far.wait_recv()
    for copy in (core_copy(0), core_copy(1), y_copy, *shares, row_y, row_core, row_far):
        copy.wait_send()

    def drain(k, c):
        req_copy(k).wait_send()
        return c

    lax.fori_loop(1, senders, drain, 0)


def front(places, marks, lengths, owners, residual_in, norm2_gain, norm2_bias, up_weight, up_bias,
          down_weight, down_bias, proj_weight, norm3_gain, norm3_bias):
    lanes, _, own_rows = places.shape
    senders = lengths.shape[0]
    width = residual_in.shape[1]
    merged = own_rows // 4
    slots = 2 * merged // senders
    pad = -(-slots // 16) * 16
    recv_rows = senders * slots
    wide = width + TAG_PAD
    hidden_own = up_weight.shape[0]
    bf16, f32 = jnp.bfloat16, jnp.float32
    small = [
        places, marks, lengths.reshape(1, -1), lengths.reshape(-1, 1), owners.reshape(-1, 1),
        norm2_gain.reshape(1, -1), norm2_bias.reshape(1, -1), up_bias.reshape(1, -1),
        down_bias.reshape(1, -1), norm3_gain.reshape(1, -1), norm3_bias.reshape(1, -1),
    ]
    large = [residual_in, up_weight, down_weight, proj_weight]
    dma = pltpu.SemaphoreType.DMA
    flops = 2 * own_rows * lanes * width * hidden_own * 2 + 2 * own_rows * width * width
    return pl.pallas_call(
        functools.partial(front_kernel, (senders, slots, pad)),
        out_shape=(
            jax.ShapeDtypeStruct((recv_rows, width), bf16),
            jax.ShapeDtypeStruct((lanes, recv_rows, wide), bf16),
        ),
        in_specs=[pl.BlockSpec(memory_space=pltpu.VMEM)] * len(small)
        + [pl.BlockSpec(memory_space=pl.ANY)] * len(large),
        out_specs=(pl.BlockSpec(memory_space=pltpu.VMEM),) * 2,
        scratch_shapes=[
            pltpu.VMEM(residual_in.shape, bf16),
            pltpu.VMEM(up_weight.shape, bf16),
            pltpu.VMEM(down_weight.shape, bf16),
            pltpu.VMEM(proj_weight.shape, bf16),
            pltpu.VMEM((own_rows, width), f32),
            pltpu.VMEM((own_rows, hidden_own), bf16),
            pltpu.VMEM((own_rows, width), f32),
            pltpu.VMEM((2, own_rows, width), bf16),
            pltpu.VMEM((2, own_rows, width), bf16),
            pltpu.VMEM((own_rows, width), bf16),
            pltpu.VMEM((own_rows, width), bf16),
            pltpu.VMEM((lanes, merged, width), bf16),
            pltpu.VMEM((lanes - 1, merged, width), bf16),
            pltpu.VMEM((senders * pad, wide), bf16),
            pltpu.VMEM((senders * pad, wide), bf16),
            dma((4,)),
            dma((2,)), dma((2,)), dma, dma,
            dma((lanes - 1,)), dma((lanes - 1,)),
            dma((senders - 1,)), dma((senders - 1,)),
            dma((3,)), dma((3,)),
        ],
        compiler_params=pltpu.CompilerParams(
            collective_id=0, has_side_effects=True, vmem_limit_bytes=VMEM_BYTES
        ),
        cost_estimate=pl.CostEstimate(flops=flops * 4, bytes_accessed=64 * 2**20, transcendentals=0),
        name="front",
    )(*small, *large)


def block_attention(heads_in, slot_tags):
    queries = heads_in[:, :, 0]
    key_rows = heads_in[:, :, 1]
    value_rows = heads_in[:, :, 2]
    score_scale = 1.0 / math.sqrt(heads_in.shape[-1])
    scores = (
        jnp.einsum("bqhe,bkhe->bhqk", queries, key_rows, preferred_element_type=jnp.float32)
        * score_scale
    )
    slot_total = heads_in.shape[1]
    itself = lax.broadcasted_iota(jnp.int32, (slot_total, slot_total), 0) == lax.broadcasted_iota(
        jnp.int32, (slot_total, slot_total), 1
    )
    live_slots = slot_tags >= 0
    same_request = slot_tags[:, :, None] == slot_tags[:, None, :]
    allowed = same_request & live_slots[:, None, :] | itself[None]
    weights = jnp.where(allowed[:, None], jnp.exp(scores), 0.0)
    probs = (weights / jnp.sum(weights, axis=-1, keepdims=True)).astype(jnp.bfloat16)
    mixed_out = jnp.einsum("bhqk,bkhe->bqhe", probs, value_rows, preferred_element_type=jnp.float32)
    mixed_out = jnp.where(live_slots[:, :, None, None], mixed_out, 0.0)
    return mixed_out.astype(jnp.bfloat16)


def body(
    residual_in,
    lengths,
    owners,
    merge_dest,
    segment_ids,
    norm2_gain,
    norm2_bias,
    up_weight,
    up_bias,
    down_weight,
    down_bias,
    proj_weight,
    norm3_gain,
    norm3_bias,
    next_weight,
):
    group_rows, model_width = residual_in.shape
    lane_count = lax.axis_size("mlp")
    sender_count = lax.axis_size("req")
    lane_index = lax.axis_index("mlp")
    own_rows = group_rows // lane_count
    merged_rows = own_rows // 4
    slot_count = 2 * merged_rows // sender_count
    part_width = model_width // lane_count
    own_columns = lax.dynamic_slice_in_dim(
        next_weight.transpose(1, 0, 2), lane_index * part_width, part_width, 2
    )
    piece = lax.all_gather(own_columns, "req", axis=1, tiled=True)
    received, everyone = front(
        merge_dest.reshape(lane_count, 1, own_rows),
        segment_ids.reshape(lane_count, 1, own_rows),
        lengths, owners, residual_in, norm2_gain, norm2_bias, up_weight, up_bias,
        down_weight, down_bias, proj_weight, norm3_gain, norm3_bias,
    )
    recv_rows = received.shape[0]
    everyone = everyone.reshape(lane_count * recv_rows, -1)
    tags = everyone[:, model_width].astype(jnp.int32).reshape(lane_count, recv_rows) - 1
    heads_in = jnp.einsum(
        "rd,sde->rse", everyone[:, :model_width], piece, preferred_element_type=jnp.float32
    )
    heads_in = heads_in.astype(jnp.bfloat16).reshape(lane_count, recv_rows, 3, -1, HEAD_DIM)
    mixed = block_attention(heads_in, tags).reshape(lane_count * recv_rows, part_width)
    next_mixed = lax.all_to_all(mixed, "mlp", split_axis=0, concat_axis=1, tiled=True)
    return (received, next_mixed)


def solution(mesh):
    return jax.shard_map(
        body,
        mesh=mesh,
        in_specs=(
            P("req", None),
            P(("req", "mlp")),
            P(("req", "mlp")),
            P("req"),
            P("req"),
            P(),
            P(),
            P("mlp", None),
            P("mlp"),
            P("mlp", None),
            P(),
            P("mlp", None),
            P(),
            P(),
            P("req", None, None),
        ),
        out_specs=(P(("req", "mlp"), None), P(("req", "mlp"), None)),
        check_vma=False,
    )
```

```python
import functools
import math

import jax
import jax.numpy as jnp
from jax import lax
from jax.experimental import pallas as pl
from jax.experimental.pallas import tpu as pltpu
from jax.sharding import PartitionSpec as P

HEAD_DIM = 104
TAG_PAD = 128
EPSILON = 1e-06


VMEM_BYTES = 56 * 2**20
MESH = pl.DeviceIdType.MESH


def front_kernel(
    sizes,
    gather,
    places_ref,
    marks_ref,
    len_row_ref,
    len_col_ref,
    own_col_ref,
    gain2_ref,
    bias2_ref,
    up_bias_ref,
    down_bias_ref,
    gain3_ref,
    bias3_ref,
    residual_hbm,
    up_hbm,
    down_hbm,
    proj_hbm,
    next_hbm,
    merged_ref,
    mixed_ref,
    everyone_ref,
    next_ref,
    mix_ref,
    residual_ref,
    up_ref,
    down_ref,
    proj_ref,
    xq_ref,
    hidden_ref,
    acc_ref,
    core_out_ref,
    core_in_ref,
    y_out_ref,
    y_in_ref,
    share_ref,
    share_in_ref,
    out_ref,
    in_ref,
    load_sem,
    core_send,
    core_recv,
    y_send,
    y_recv,
    share_send,
    share_recv,
    req_send,
    req_recv,
    all_send,
    all_recv,
    next_send,
    next_recv,
    mix_send,
    mix_recv,
):
    senders, slots, pad = sizes
    lanes = 4
    m = lax.axis_index("mlp")
    r = lax.axis_index("req")
    core_peer = m + 1 - 2 * (m % 2)
    y_peer = (m + 2) % lanes
    own_rows = places_ref.shape[-1]
    merged = own_rows // 4
    width = residual_ref.shape[1]
    wide = out_ref.shape[1]
    shard_rows = next_hbm.shape[0]
    heights = senders // 2
    x_peer = r + 1 - 2 * (r % 2)

    def shard(index):
        return pl.ds(pl.multiple_of(index * shard_rows, 16), shard_rows)

    def next_copy(slot, index, peer):
        return pltpu.make_async_remote_copy(
            src_ref=next_ref.at[shard(index)], dst_ref=next_ref.at[shard(index)],
            send_sem=next_send.at[slot], recv_sem=next_recv.at[slot],
            device_id={"req": peer}, device_id_type=MESH,
        )

    def z_copy(k):
        return next_copy(k, r, (r + 2 * k) % senders)

    def forward(k):
        return next_copy(heights - 1 + k, (r + senders - 2 * k) % senders, x_peer)

    def pass_on(k):
        if gather:
            z_copy(k).wait_recv()
            forward(k).start()


    loads = [
        pltpu.make_async_copy(a, b, load_sem.at[i])
        for i, (a, b) in enumerate(
            (
                (residual_hbm, residual_ref), (up_hbm, up_ref), (down_hbm, down_ref), (proj_hbm, proj_ref),
                (next_hbm, next_ref.at[shard(r)] if gather else next_ref),
            )
        )
    ]
    for load in loads:
        load.start()

    barrier = pltpu.get_barrier_semaphore()
    for k in range(1, lanes):
        pl.semaphore_signal(barrier, inc=1, device_id={"mlp": (m + k) % lanes}, device_id_type=MESH)

    def greet(k, c):
        pl.semaphore_signal(barrier, inc=1, device_id={"req": (r + k) % senders}, device_id_type=MESH)
        return c

    lax.fori_loop(1, senders, greet, 0)
    pl.semaphore_wait(barrier, lanes - 1 + senders - 1)

    def norm(values, gain, bias):
        mean_value = jnp.mean(values, axis=-1, keepdims=True)
        centred = values - mean_value
        spread = jnp.mean(centred * centred, axis=-1, keepdims=True)
        return centred * lax.rsqrt(spread + EPSILON) * gain + bias

    def core_copy(i):
        return pltpu.make_async_remote_copy(
            src_ref=core_out_ref.at[i], dst_ref=core_in_ref.at[i],
            send_sem=core_send.at[i], recv_sem=core_recv.at[i],
            device_id={"mlp": core_peer}, device_id_type=MESH,
        )

    y_copy = pltpu.make_async_remote_copy(
        src_ref=y_out_ref, dst_ref=y_in_ref, send_sem=y_send, recv_sem=y_recv,
        device_id={"mlp": y_peer}, device_id_type=MESH,
    )

    if gather:
        loads[4].wait()
        next_copy(0, r, x_peer).start()
        for k in range(1, heights):
            z_copy(k).start()

    loads[0].wait()

    def quadrant_step(step, c):
        first = 1 - step // 2
        second = 1 - step % 2
        q = (1 - second) * m + second * core_peer
        q = (1 - first) * q + first * ((q + 2) % lanes)
        want = 4 * lax.broadcasted_iota(jnp.int32, (merged, own_rows), 0) + q
        for b in range(lanes):
            hits = (want == places_ref[b]).astype(jnp.float32).astype(jnp.bfloat16)
            xq_ref[b * merged : (b + 1) * merged, :] = jnp.dot(
                hits,
                residual_ref[b * own_rows : (b + 1) * own_rows, :],
                preferred_element_type=jnp.float32,
            )
        normed = norm(xq_ref[...], gain2_ref[...], bias2_ref[...]).astype(jnp.bfloat16)

        @pl.when(step == 0)
        def _():
            loads[1].wait()

        hidden_total = up_ref.shape[0]
        for j in range(0, hidden_total, 256):
            upward = lax.dot_general(
                normed, up_ref[j : j + 256, :], (((1,), (1,)), ((), ())),
                preferred_element_type=jnp.float32,
            ) + up_bias_ref[:, j : j + 256]
            hidden_ref[:, j : j + 256] = (
                0.5 * upward * (1.0 + lax.erf(upward * math.sqrt(0.5)))
            ).astype(jnp.bfloat16)

        @pl.when(step == 0)
        def _():
            loads[2].wait()

        acc_ref[...] = jnp.dot(hidden_ref[...], down_ref[...], preferred_element_type=jnp.float32)

        @pl.when(step == 0)
        def _():
            core_out_ref[0] = acc_ref[...].astype(jnp.bfloat16)
            core_copy(0).start()

        @pl.when(step == 1)
        def _():
            core_copy(0).wait_recv()
            y_out_ref[...] = (acc_ref[...] + core_in_ref[0].astype(jnp.float32)).astype(jnp.bfloat16)
            y_copy.start()

        @pl.when(step == 2)
        def _():
            core_out_ref[1] = acc_ref[...].astype(jnp.bfloat16)
            core_copy(1).start()

        return c

    lax.fori_loop(0, lanes, quadrant_step, 0)
    counts_row = len_row_ref[...] // 4
    counts_col = len_col_ref[...] // 4
    before = (
        lax.broadcasted_iota(jnp.int32, (senders, senders), 1)
        < lax.broadcasted_iota(jnp.int32, (senders, senders), 0)
    )
    starts = jnp.sum(jnp.where(before, counts_row, 0), axis=1, keepdims=True)
    index = lax.broadcasted_iota(jnp.int32, (senders, merged), 1)
    inside = (index >= starts) & (index < starts + counts_col)
    owner_of = jnp.sum(jnp.where(inside, own_col_ref[...], 0), axis=0, keepdims=True)
    begun = jnp.sum(jnp.where(inside, starts, 0), axis=0, keepdims=True)
    target = owner_of * pad + index[0:1, :] - begun
    route = (
        lax.broadcasted_iota(jnp.int32, (senders * pad, merged), 0) == target
    ).astype(jnp.float32).astype(jnp.bfloat16)
    first_hits = 4 * lax.broadcasted_iota(jnp.int32, (merged, own_rows), 0) == places_ref[m]
    row_tag = 1 + jnp.sum(jnp.where(first_hits, marks_ref[m], 0), axis=1, keepdims=True)
    tag_columns = jnp.broadcast_to(row_tag.astype(jnp.float32), (merged, wide - width))

    core_copy(1).wait_recv()
    y_copy.wait_recv()
    layer_out = (
        xq_ref[...] + (acc_ref[...] + core_in_ref[1].astype(jnp.float32) + y_in_ref[...].astype(jnp.float32))
        + down_bias_ref[...]
    ).astype(jnp.bfloat16)
    loads[3].wait()
    acc_ref[...] = jnp.dot(layer_out, proj_ref[...], preferred_element_type=jnp.float32)
    for b in range(lanes):
        share_ref[b] = acc_ref[b * merged : (b + 1) * merged, :].astype(jnp.bfloat16)
    shares = [
        pltpu.make_async_remote_copy(
            src_ref=share_ref.at[(m + k) % lanes], dst_ref=share_in_ref.at[k - 1],
            send_sem=share_send.at[k - 1], recv_sem=share_recv.at[k - 1],
            device_id={"mlp": (m + k) % lanes}, device_id_type=MESH,
        )
        for k in range(1, lanes)
    ]
    for share in shares:
        share.start()
    for k in range(1, heights, 2):
        pass_on(k)
    for share in shares:
        share.wait_recv()
    total = share_ref[m].astype(jnp.float32)
    for k in range(1, lanes):
        total = total + share_in_ref[k - 1].astype(jnp.float32)
    extended = jnp.concatenate([total, tag_columns], axis=1).astype(jnp.bfloat16)
    out_ref[...] = jnp.dot(route, extended, preferred_element_type=jnp.float32).astype(jnp.bfloat16)

    def req_copy(k):
        to = (r + k) % senders
        return pltpu.make_async_remote_copy(
            src_ref=out_ref.at[pl.ds(pl.multiple_of(to * pad, 16), pad)],
            dst_ref=in_ref.at[pl.ds(pl.multiple_of(r * pad, 16), pad)],
            send_sem=req_send.at[k - 1], recv_sem=req_recv.at[k - 1],
            device_id={"req": to}, device_id_type=MESH,
        )

    def start_req(k, c):
        req_copy(k).start()
        return c

    lax.fori_loop(1, senders, start_req, 0)
    for k in range(2, heights, 2):
        pass_on(k)
    own = pl.ds(pl.multiple_of(r * pad, 16), pad)
    in_ref[own, :] = out_ref[own, :]
    def wait_req(k, c):
        req_copy(k).wait_recv()
        return c

    lax.fori_loop(1, senders, wait_req, 0)
    arrived = in_ref[...]
    if pad != slots:
        row = lax.broadcasted_iota(jnp.int32, (senders * slots, senders * pad), 0)
        column = lax.broadcasted_iota(jnp.int32, (senders * slots, senders * pad), 1)
        pick = (row // slots * pad + row % slots == column).astype(jnp.float32).astype(jnp.bfloat16)
        arrived = jnp.dot(pick, arrived, preferred_element_type=jnp.float32).astype(jnp.bfloat16)
    received = arrived[:, :width]
    merged_ref[...] = received
    everyone_ref[m, :, width:] = arrived[:, width:]
    everyone_ref[m, :, :width] = norm(
        received.astype(jnp.float32), gain3_ref[...], bias3_ref[...]
    ).astype(jnp.bfloat16)

    def row_copy(slot, block, peer):
        return pltpu.make_async_remote_copy(
            src_ref=everyone_ref.at[block], dst_ref=everyone_ref.at[block],
            send_sem=all_send.at[slot], recv_sem=all_recv.at[slot],
            device_id={"mlp": peer}, device_id_type=MESH,
        )

    row_y = row_copy(0, m, y_peer)
    row_core = row_copy(1, m, core_peer)
    row_y.start()
    row_core.start()
    if gather:
        for k in range(heights):
            if k:
                forward(k).wait_recv()
            else:
                next_copy(0, r, x_peer).wait_recv()
    else:
        loads[4].wait()
    part = next_ref.shape[1] // 3
    score_scale = 1.0 / math.sqrt(HEAD_DIM)
    recv_rows = senders * slots
    itself = lax.broadcasted_iota(jnp.int32, (recv_rows, recv_rows), 0) == lax.broadcasted_iota(
        jnp.int32, (recv_rows, recv_rows), 1
    )
    row_far = row_copy(2, y_peer, core_peer)

    def block_of(step):
        first = step // 2
        second = step % 2
        block = (1 - second) * m + second * core_peer
        return (1 - first) * block + first * ((block + 2) % lanes)

    def mix_copy(step):
        return pltpu.make_async_remote_copy(
            src_ref=mix_ref.at[block_of(step)], dst_ref=mixed_ref.at[m],
            send_sem=mix_send.at[step - 1], recv_sem=mix_recv.at[step - 1],
            device_id={"mlp": block_of(step)}, device_id_type=MESH,
        )

    def attend(step, c):
        @pl.when(step == 1)
        def _():
            row_core.wait_recv()

        @pl.when(step == 2)
        def _():
            row_y.wait_recv()
            row_far.start()

        @pl.when(step == 3)
        def _():
            row_far.wait_recv()

        block = block_of(step)
        rows = everyone_ref[block]
        heads = jnp.dot(rows[:, :width], next_ref[...], preferred_element_type=jnp.float32)
        tags = rows[:, width : width + recv_rows].astype(jnp.float32)
        key_tags = tags.T
        allowed = ((tags == key_tags) & (key_tags > 0.5)) | itself
        live = tags[:, :1] > 0.5
        outs = []
        for h in range(part // HEAD_DIM):
            at = h * HEAD_DIM
            query, key, value = (
                heads[:, i * part + at : i * part + at + HEAD_DIM].astype(jnp.bfloat16) for i in range(3)
            )
            scores = lax.dot_general(
                query, key, (((1,), (1,)), ((), ())), preferred_element_type=jnp.float32
            ) * score_scale
            weights = jnp.where(allowed, jnp.exp(scores), 0.0)
            probs = (weights / jnp.sum(weights, axis=-1, keepdims=True)).astype(jnp.bfloat16)
            mixed = jnp.dot(probs, value, preferred_element_type=jnp.float32)
            outs.append(jnp.where(live, mixed, 0.0))
        mix_ref[block] = jnp.concatenate(outs, axis=1).astype(jnp.bfloat16)

        @pl.when(step > 0)
        def _():
            mix_copy(step).start()

        return c

    lax.fori_loop(0, lanes, attend, 0)
    mixed_ref[m] = mix_ref[m]
    for step in range(1, lanes):
        mix_copy(step).wait()
    for copy in (core_copy(0), core_copy(1), y_copy, *shares, row_y, row_core, row_far):
        copy.wait_send()

    def drain(k, c):
        req_copy(k).wait_send()
        return c

    lax.fori_loop(1, senders, drain, 0)
    if gather:
        next_copy(0, r, x_peer).wait_send()
        for k in range(1, heights):
            z_copy(k).wait_send()
            forward(k).wait_send()


def front(places, marks, lengths, owners, residual_in, norm2_gain, norm2_bias, up_weight, up_bias,
          down_weight, down_bias, proj_weight, norm3_gain, norm3_bias, next_part, gather):
    lanes, _, own_rows = places.shape
    senders = lengths.shape[0]
    width = residual_in.shape[1]
    merged = own_rows // 4
    slots = 2 * merged // senders
    pad = -(-slots // 16) * 16
    recv_rows = senders * slots
    wide = width + TAG_PAD
    hidden_own = up_weight.shape[0]
    bf16, f32 = jnp.bfloat16, jnp.float32
    small = [
        places, marks, lengths.reshape(1, -1), lengths.reshape(-1, 1), owners.reshape(-1, 1),
        norm2_gain.reshape(1, -1), norm2_bias.reshape(1, -1), up_bias.reshape(1, -1),
        down_bias.reshape(1, -1), norm3_gain.reshape(1, -1), norm3_bias.reshape(1, -1),
    ]
    large = [residual_in, up_weight, down_weight, proj_weight, next_part]
    dma = pltpu.SemaphoreType.DMA
    flops = 2 * own_rows * lanes * width * hidden_own * 2 + 2 * own_rows * width * width
    return pl.pallas_call(
        functools.partial(front_kernel, (senders, slots, pad), gather),
        out_shape=(
            jax.ShapeDtypeStruct((recv_rows, width), bf16),
            jax.ShapeDtypeStruct((lanes, recv_rows, next_part.shape[1] // 3), bf16),
        ),
        in_specs=[pl.BlockSpec(memory_space=pltpu.VMEM)] * len(small)
        + [pl.BlockSpec(memory_space=pl.ANY)] * len(large),
        out_specs=(pl.BlockSpec(memory_space=pltpu.VMEM),) * 2,
        scratch_shapes=[
            pltpu.VMEM((lanes, recv_rows, wide), bf16),
            pltpu.VMEM((width, next_part.shape[1]), bf16),
            pltpu.VMEM((lanes, recv_rows, next_part.shape[1] // 3), bf16),
            pltpu.VMEM(residual_in.shape, bf16),
            pltpu.VMEM(up_weight.shape, bf16),
            pltpu.VMEM(down_weight.shape, bf16),
            pltpu.VMEM(proj_weight.shape, bf16),
            pltpu.VMEM((own_rows, width), f32),
            pltpu.VMEM((own_rows, hidden_own), bf16),
            pltpu.VMEM((own_rows, width), f32),
            pltpu.VMEM((2, own_rows, width), bf16),
            pltpu.VMEM((2, own_rows, width), bf16),
            pltpu.VMEM((own_rows, width), bf16),
            pltpu.VMEM((own_rows, width), bf16),
            pltpu.VMEM((lanes, merged, width), bf16),
            pltpu.VMEM((lanes - 1, merged, width), bf16),
            pltpu.VMEM((senders * pad, wide), bf16),
            pltpu.VMEM((senders * pad, wide), bf16),
            dma((5,)),
            dma((2,)), dma((2,)), dma, dma,
            dma((lanes - 1,)), dma((lanes - 1,)),
            dma((senders - 1,)), dma((senders - 1,)),
            dma((3,)), dma((3,)),
            dma((senders - 1,)), dma((senders - 1,)),
            dma((lanes - 1,)), dma((lanes - 1,)),
        ],
        compiler_params=pltpu.CompilerParams(
            collective_id=0, has_side_effects=True, vmem_limit_bytes=VMEM_BYTES
        ),
        cost_estimate=pl.CostEstimate(flops=flops * 4, bytes_accessed=64 * 2**20, transcendentals=0),
        name="front",
    )(*small, *large)


def body(
    residual_in,
    lengths,
    owners,
    merge_dest,
    segment_ids,
    norm2_gain,
    norm2_bias,
    up_weight,
    up_bias,
    down_weight,
    down_bias,
    proj_weight,
    norm3_gain,
    norm3_bias,
    next_weight,
):
    group_rows, model_width = residual_in.shape
    lane_count = lax.axis_size("mlp")
    lane_index = lax.axis_index("mlp")
    own_rows = group_rows // lane_count
    part_width = model_width // lane_count
    own_columns = lax.dynamic_slice_in_dim(
        next_weight, lane_index * part_width, part_width, 2
    ).reshape(next_weight.shape[0], -1)
    gather = next_weight.shape[0] % 16 == 0
    if not gather:
        own_columns = lax.all_gather(own_columns, "req", axis=0, tiled=True)
    received, mixed = front(
        merge_dest.reshape(lane_count, 1, own_rows),
        segment_ids.reshape(lane_count, 1, own_rows),
        lengths, owners, residual_in, norm2_gain, norm2_bias, up_weight, up_bias,
        down_weight, down_bias, proj_weight, norm3_gain, norm3_bias, own_columns, gather,
    )
    next_mixed = mixed.transpose(1, 0, 2).reshape(received.shape)
    return (received, next_mixed)


def solution(mesh):
    return jax.shard_map(
        body,
        mesh=mesh,
        in_specs=(
            P("req", None),
            P(("req", "mlp")),
            P(("req", "mlp")),
            P("req"),
            P("req"),
            P(),
            P(),
            P("mlp", None),
            P("mlp"),
            P("mlp", None),
            P(),
            P("mlp", None),
            P(),
            P(),
            P("req", None, None),
        ),
        out_specs=(P(("req", "mlp"), None), P(("req", "mlp"), None)),
        check_vma=False,
    )
```

```python
import functools
import math

import jax
import jax.numpy as jnp
from jax import lax
from jax.experimental import pallas as pl
from jax.experimental.pallas import tpu as pltpu
from jax.sharding import PartitionSpec as P

HEAD_DIM = 104
TAG_PAD = 128
EPSILON = 1e-06


VMEM_BYTES = 56 * 2**20
MESH = pl.DeviceIdType.MESH


def front_kernel(
    sizes,
    gather,
    places_ref,
    marks_ref,
    len_ref,
    owner_ref,
    up_bias_ref,
    params_ref,
    residual_hbm,
    up_hbm,
    down_hbm,
    proj_hbm,
    next_hbm,
    merged_ref,
    next_mixed_ref,
    mixed_ref,
    everyone_ref,
    next_ref,
    mix_ref,
    residual_ref,
    up_ref,
    down_ref,
    proj_ref,
    xq_ref,
    hidden_ref,
    acc_ref,
    core_out_ref,
    core_in_ref,
    y_out_ref,
    y_in_ref,
    share_ref,
    share_out_ref,
    share_in_ref,
    out_ref,
    in_ref,
    load_sem,
    core_send,
    core_recv,
    y_send,
    y_recv,
    share_send,
    share_recv,
    req_send,
    req_recv,
    all_send,
    all_recv,
    next_send,
    next_recv,
    mix_send,
    mix_recv,
):
    senders, slots, pad = sizes
    lanes = 4
    m = lax.axis_index("mlp")
    r = lax.axis_index("req")
    core_peer = m + 1 - 2 * (m % 2)
    y_peer = (m + 2) % lanes
    own_rows = places_ref.shape[-1]
    merged = own_rows // 4
    width = residual_ref.shape[1]
    wide = out_ref.shape[1]
    shard_rows = next_hbm.shape[0]
    heights = senders // 2
    x_peer = r + 1 - 2 * (r % 2)

    def shard(index):
        return pl.ds(pl.multiple_of(index * shard_rows, 16), shard_rows)

    def next_copy(slot, index, peer):
        return pltpu.make_async_remote_copy(
            src_ref=next_ref.at[shard(index)], dst_ref=next_ref.at[shard(index)],
            send_sem=next_send.at[slot], recv_sem=next_recv.at[slot],
            device_id={"req": peer}, device_id_type=MESH,
        )

    def z_copy(k):
        return next_copy(k, r, (r + 2 * k) % senders)

    def forward(k):
        return next_copy(heights - 1 + k, (r + senders - 2 * k) % senders, x_peer)

    def pass_on(k):
        if gather:
            z_copy(k).wait_recv()
            forward(k).start()


    loads = [
        pltpu.make_async_copy(a, b, load_sem.at[i])
        for i, (a, b) in enumerate(
            (
                (residual_hbm, residual_ref), (up_hbm, up_ref), (down_hbm, down_ref), (proj_hbm, proj_ref),
                (next_hbm, next_ref.at[shard(r)] if gather else next_ref),
            )
        )
    ]
    for load in loads:
        load.start()

    barrier = pltpu.get_barrier_semaphore()
    for k in range(1, lanes):
        pl.semaphore_signal(barrier, inc=1, device_id={"mlp": (m + k) % lanes}, device_id_type=MESH)

    def greet(k, c):
        pl.semaphore_signal(barrier, inc=1, device_id={"req": (r + k) % senders}, device_id_type=MESH)
        return c

    lax.fori_loop(1, senders, greet, 0)
    pl.semaphore_wait(barrier, lanes - 1 + senders - 1)

    def norm(values, gain, bias):
        mean_value = jnp.mean(values, axis=-1, keepdims=True)
        centred = values - mean_value
        spread = jnp.mean(centred * centred, axis=-1, keepdims=True)
        return centred * lax.rsqrt(spread + EPSILON) * gain + bias

    def core_copy(i):
        return pltpu.make_async_remote_copy(
            src_ref=core_out_ref.at[i], dst_ref=core_in_ref.at[i],
            send_sem=core_send.at[i], recv_sem=core_recv.at[i],
            device_id={"mlp": core_peer}, device_id_type=MESH,
        )

    y_copy = pltpu.make_async_remote_copy(
        src_ref=y_out_ref, dst_ref=y_in_ref, send_sem=y_send, recv_sem=y_recv,
        device_id={"mlp": y_peer}, device_id_type=MESH,
    )

    if gather:
        loads[4].wait()
        next_copy(0, r, x_peer).start()
        for k in range(1, heights, 2):
            z_copy(k).start()

    loads[0].wait()

    def quadrant_step(step, c):
        if gather:
            @pl.when(step == 1)
            def _():
                for k in range(2, heights, 2):
                    z_copy(k).start()

            @pl.when(step == 2)
            def _():
                pass_on(1)

            @pl.when(step == 3)
            def _():
                for k in range(3, heights, 2):
                    pass_on(k)

        first = 1 - step // 2
        second = 1 - step % 2
        q = (1 - second) * m + second * core_peer
        q = (1 - first) * q + first * ((q + 2) % lanes)
        want = 4 * lax.broadcasted_iota(jnp.int32, (merged, own_rows), 0) + q
        for b in range(lanes):
            hits = (want == places_ref[b]).astype(jnp.float32).astype(jnp.bfloat16)
            xq_ref[b * merged : (b + 1) * merged, :] = jnp.dot(
                hits,
                residual_ref[b * own_rows : (b + 1) * own_rows, :],
                preferred_element_type=jnp.float32,
            )
        normed = norm(xq_ref[...], params_ref[0:1, :], params_ref[1:2, :]).astype(jnp.bfloat16)

        @pl.when(step == 0)
        def _():
            loads[1].wait()

        hidden_total = up_ref.shape[0]
        for j in range(0, hidden_total, 256):
            upward = lax.dot_general(
                normed, up_ref[j : j + 256, :], (((1,), (1,)), ((), ())),
                preferred_element_type=jnp.float32,
            ) + up_bias_ref[:, j : j + 256]
            hidden_ref[:, j : j + 256] = (
                0.5 * upward * (1.0 + lax.erf(upward * math.sqrt(0.5)))
            ).astype(jnp.bfloat16)

        @pl.when(step == 0)
        def _():
            loads[2].wait()

        acc_ref[...] = jnp.dot(hidden_ref[...], down_ref[...], preferred_element_type=jnp.float32)

        @pl.when(step == 0)
        def _():
            core_out_ref[0] = acc_ref[...].astype(jnp.bfloat16)
            core_copy(0).start()

        @pl.when(step == 1)
        def _():
            core_copy(0).wait_recv()
            y_out_ref[...] = (acc_ref[...] + core_in_ref[0].astype(jnp.float32)).astype(jnp.bfloat16)
            y_copy.start()

        @pl.when(step == 2)
        def _():
            core_out_ref[1] = acc_ref[...].astype(jnp.bfloat16)
            core_copy(1).start()

        return c

    lax.fori_loop(0, lanes, quadrant_step, 0)
    counts_row = len_ref[...] // 4
    down_index = lax.broadcasted_iota(jnp.int32, (senders, senders), 0)
    across_index = lax.broadcasted_iota(jnp.int32, (senders, senders), 1)
    counts_col = jnp.sum(
        jnp.where(across_index == down_index, counts_row, 0), axis=1, keepdims=True
    )
    owners_col = jnp.sum(
        jnp.where(across_index == down_index, owner_ref[...], 0), axis=1, keepdims=True
    )
    before = across_index < down_index
    starts = jnp.sum(jnp.where(before, counts_row, 0), axis=1, keepdims=True)
    index = lax.broadcasted_iota(jnp.int32, (senders, merged), 1)
    inside = (index >= starts) & (index < starts + counts_col)
    owner_of = jnp.sum(jnp.where(inside, owners_col, 0), axis=0, keepdims=True)
    begun = jnp.sum(jnp.where(inside, starts, 0), axis=0, keepdims=True)
    target = owner_of * pad + index[0:1, :] - begun
    route = (
        lax.broadcasted_iota(jnp.int32, (senders * pad, merged), 0) == target
    ).astype(jnp.float32).astype(jnp.bfloat16)
    first_hits = 4 * lax.broadcasted_iota(jnp.int32, (merged, own_rows), 0) == places_ref[m]
    row_tag = 1 + jnp.sum(jnp.where(first_hits, marks_ref[m], 0), axis=1, keepdims=True)
    tag_columns = jnp.broadcast_to(row_tag.astype(jnp.float32), (merged, wide - width))

    core_copy(1).wait_recv()
    y_copy.wait_recv()
    layer_out = (
        xq_ref[...] + (acc_ref[...] + core_in_ref[1].astype(jnp.float32) + y_in_ref[...].astype(jnp.float32))
        + params_ref[2:3, :]
    ).astype(jnp.bfloat16)
    loads[3].wait()
    acc_ref[...] = jnp.dot(layer_out, proj_ref[...], preferred_element_type=jnp.float32)
    for b in range(lanes):
        share_ref[b] = acc_ref[b * merged : (b + 1) * merged, :].astype(jnp.bfloat16)
    far = lanes - 1 - m

    def share_copy(slot, source, peer):
        return pltpu.make_async_remote_copy(
            src_ref=source, dst_ref=share_in_ref.at[slot],
            send_sem=share_send.at[slot], recv_sem=share_recv.at[slot],
            device_id={"mlp": peer}, device_id_type=MESH,
        )

    share_y = share_copy(2, share_out_ref, y_peer)
    shares = [
        share_copy(0, share_ref.at[far], core_peer),
        share_copy(1, share_ref.at[core_peer], core_peer),
        share_y,
    ]
    shares[0].start()
    shares[1].start()
    shares[0].wait_recv()
    share_out_ref[...] = (
        share_ref[y_peer].astype(jnp.float32) + share_in_ref[0].astype(jnp.float32)
    ).astype(jnp.bfloat16)
    share_y.start()
    for k in range(2, heights, 2):
        pass_on(k)
    shares[1].wait_recv()
    total = share_ref[m].astype(jnp.float32) + share_in_ref[1].astype(jnp.float32)
    share_y.wait_recv()
    total = total + share_in_ref[2].astype(jnp.float32)
    extended = jnp.concatenate([total, tag_columns], axis=1).astype(jnp.bfloat16)
    out_ref[...] = jnp.dot(route, extended, preferred_element_type=jnp.float32).astype(jnp.bfloat16)

    def req_copy(k):
        to = (r + k) % senders
        return pltpu.make_async_remote_copy(
            src_ref=out_ref.at[pl.ds(pl.multiple_of(to * pad, 16), pad)],
            dst_ref=in_ref.at[pl.ds(pl.multiple_of(r * pad, 16), pad)],
            send_sem=req_send.at[k - 1], recv_sem=req_recv.at[k - 1],
            device_id={"req": to}, device_id_type=MESH,
        )

    def start_req(k, c):
        req_copy(k).start()
        return c

    lax.fori_loop(1, senders, start_req, 0)
    own = pl.ds(pl.multiple_of(r * pad, 16), pad)
    in_ref[own, :] = out_ref[own, :]
    def wait_req(k, c):
        req_copy(k).wait_recv()
        return c

    lax.fori_loop(1, senders, wait_req, 0)
    arrived = in_ref[...]
    if pad != slots:
        row = lax.broadcasted_iota(jnp.int32, (senders * slots, senders * pad), 0)
        column = lax.broadcasted_iota(jnp.int32, (senders * slots, senders * pad), 1)
        pick = (row // slots * pad + row % slots == column).astype(jnp.float32).astype(jnp.bfloat16)
        arrived = jnp.dot(pick, arrived, preferred_element_type=jnp.float32).astype(jnp.bfloat16)
    received = arrived[:, :width]
    merged_ref[...] = received
    everyone_ref[m, :, width:] = arrived[:, width:]
    everyone_ref[m, :, :width] = norm(
        received.astype(jnp.float32), params_ref[3:4, :], params_ref[4:5, :]
    ).astype(jnp.bfloat16)

    def row_copy(slot, block, peer):
        return pltpu.make_async_remote_copy(
            src_ref=everyone_ref.at[block], dst_ref=everyone_ref.at[block],
            send_sem=all_send.at[slot], recv_sem=all_recv.at[slot],
            device_id={"mlp": peer}, device_id_type=MESH,
        )

    row_y = row_copy(0, m, y_peer)
    row_core = row_copy(1, m, core_peer)
    row_y.start()
    row_core.start()
    if gather:
        for k in range(heights):
            if k:
                forward(k).wait_recv()
            else:
                next_copy(0, r, x_peer).wait_recv()
    else:
        loads[4].wait()
    part = next_ref.shape[1] // 3
    score_scale = 1.0 / math.sqrt(HEAD_DIM)
    recv_rows = senders * slots
    itself = lax.broadcasted_iota(jnp.int32, (recv_rows, recv_rows), 0) == lax.broadcasted_iota(
        jnp.int32, (recv_rows, recv_rows), 1
    )
    row_far = row_copy(2, y_peer, core_peer)

    def block_of(step):
        first = step // 2
        second = step % 2
        block = (1 - second) * m + second * core_peer
        return (1 - first) * block + first * ((block + 2) % lanes)

    def mix_copy(step):
        return pltpu.make_async_remote_copy(
            src_ref=mix_ref.at[block_of(step)], dst_ref=mixed_ref.at[m],
            send_sem=mix_send.at[step - 1], recv_sem=mix_recv.at[step - 1],
            device_id={"mlp": block_of(step)}, device_id_type=MESH,
        )

    def attend(step, c):
        @pl.when(step == 1)
        def _():
            row_core.wait_recv()

        @pl.when(step == 2)
        def _():
            row_y.wait_recv()
            row_far.start()

        @pl.when(step == 3)
        def _():
            row_far.wait_recv()

        block = block_of(step)
        rows = everyone_ref[block]
        heads = jnp.dot(rows[:, :width], next_ref[...], preferred_element_type=jnp.float32)
        tags = rows[:, width : width + recv_rows].astype(jnp.float32)
        key_tags = tags.T
        allowed = ((tags == key_tags) & (key_tags > 0.5)) | itself
        live = tags[:, :1] > 0.5
        outs = []
        for h in range(part // HEAD_DIM):
            at = h * HEAD_DIM
            query, key, value = (
                heads[:, i * part + at : i * part + at + HEAD_DIM].astype(jnp.bfloat16) for i in range(3)
            )
            scores = lax.dot_general(
                query, key, (((1,), (1,)), ((), ())), preferred_element_type=jnp.float32
            ) * score_scale
            weights = jnp.where(allowed, jnp.exp(scores), 0.0)
            probs = (weights / jnp.sum(weights, axis=-1, keepdims=True)).astype(jnp.bfloat16)
            mixed = jnp.dot(probs, value, preferred_element_type=jnp.float32)
            outs.append(jnp.where(live, mixed, 0.0))
        mix_ref[block] = jnp.concatenate(outs, axis=1).astype(jnp.bfloat16)

        @pl.when(step > 0)
        def _():
            mix_copy(step).start()

        return c

    lax.fori_loop(0, lanes, attend, 0)
    mixed_ref[m] = mix_ref[m]
    for step in range(1, lanes):
        mix_copy(step).wait()
    next_mixed_ref[...] = jnp.concatenate(
        [mixed_ref[b].astype(jnp.float32) for b in range(lanes)], axis=1
    ).astype(jnp.bfloat16)
    for copy in (core_copy(0), core_copy(1), y_copy, *shares, row_y, row_core, row_far):
        copy.wait_send()

    def drain(k, c):
        req_copy(k).wait_send()
        return c

    lax.fori_loop(1, senders, drain, 0)
    if gather:
        next_copy(0, r, x_peer).wait_send()
        for k in range(1, heights):
            z_copy(k).wait_send()
            forward(k).wait_send()


def front(places, marks, lengths, owners, residual_in, norm2_gain, norm2_bias, up_weight, up_bias,
          down_weight, down_bias, proj_weight, norm3_gain, norm3_bias, next_part, gather):
    lanes, _, own_rows = places.shape
    senders = lengths.shape[0]
    width = residual_in.shape[1]
    merged = own_rows // 4
    slots = 2 * merged // senders
    pad = -(-slots // 16) * 16
    recv_rows = senders * slots
    wide = width + TAG_PAD
    hidden_own = up_weight.shape[0]
    bf16, f32 = jnp.bfloat16, jnp.float32
    small = [
        places, marks, lengths.reshape(1, -1), owners.reshape(1, -1), up_bias.reshape(1, -1),
        jnp.stack([norm2_gain, norm2_bias, down_bias, norm3_gain, norm3_bias]),
    ]
    large = [residual_in, up_weight, down_weight, proj_weight, next_part]
    dma = pltpu.SemaphoreType.DMA
    flops = 2 * own_rows * lanes * width * hidden_own * 2 + 2 * own_rows * width * width
    return pl.pallas_call(
        functools.partial(front_kernel, (senders, slots, pad), gather),
        out_shape=(
            jax.ShapeDtypeStruct((recv_rows, width), bf16),
            jax.ShapeDtypeStruct((recv_rows, width), bf16),
        ),
        in_specs=[pl.BlockSpec(memory_space=pltpu.VMEM)] * len(small)
        + [pl.BlockSpec(memory_space=pl.ANY)] * len(large),
        out_specs=(pl.BlockSpec(memory_space=pltpu.VMEM),) * 2,
        scratch_shapes=[
            pltpu.VMEM((lanes, recv_rows, next_part.shape[1] // 3), bf16),
            pltpu.VMEM((lanes, recv_rows, wide), bf16),
            pltpu.VMEM((width, next_part.shape[1]), bf16),
            pltpu.VMEM((lanes, recv_rows, next_part.shape[1] // 3), bf16),
            pltpu.VMEM(residual_in.shape, bf16),
            pltpu.VMEM(up_weight.shape, bf16),
            pltpu.VMEM(down_weight.shape, bf16),
            pltpu.VMEM(proj_weight.shape, bf16),
            pltpu.VMEM((own_rows, width), f32),
            pltpu.VMEM((own_rows, hidden_own), bf16),
            pltpu.VMEM((own_rows, width), f32),
            pltpu.VMEM((2, own_rows, width), bf16),
            pltpu.VMEM((2, own_rows, width), bf16),
            pltpu.VMEM((own_rows, width), bf16),
            pltpu.VMEM((own_rows, width), bf16),
            pltpu.VMEM((lanes, merged, width), bf16),
            pltpu.VMEM((merged, width), bf16),
            pltpu.VMEM((lanes - 1, merged, width), bf16),
            pltpu.VMEM((senders * pad, wide), bf16),
            pltpu.VMEM((senders * pad, wide), bf16),
            dma((5,)),
            dma((2,)), dma((2,)), dma, dma,
            dma((lanes - 1,)), dma((lanes - 1,)),
            dma((senders - 1,)), dma((senders - 1,)),
            dma((3,)), dma((3,)),
            dma((senders - 1,)), dma((senders - 1,)),
            dma((lanes - 1,)), dma((lanes - 1,)),
        ],
        compiler_params=pltpu.CompilerParams(
            collective_id=0, has_side_effects=True, vmem_limit_bytes=VMEM_BYTES
        ),
        cost_estimate=pl.CostEstimate(flops=flops * 4, bytes_accessed=64 * 2**20, transcendentals=0),
        name="front",
    )(*small, *large)


def body(
    residual_in,
    lengths,
    owners,
    merge_dest,
    segment_ids,
    norm2_gain,
    norm2_bias,
    up_weight,
    up_bias,
    down_weight,
    down_bias,
    proj_weight,
    norm3_gain,
    norm3_bias,
    next_weight,
):
    group_rows, model_width = residual_in.shape
    lane_count = lax.axis_size("mlp")
    lane_index = lax.axis_index("mlp")
    own_rows = group_rows // lane_count
    part_width = model_width // lane_count
    own_columns = lax.dynamic_slice_in_dim(
        next_weight, lane_index * part_width, part_width, 2
    ).reshape(next_weight.shape[0], -1)
    gather = next_weight.shape[0] % 16 == 0
    if not gather:
        own_columns = lax.all_gather(own_columns, "req", axis=0, tiled=True)
    return front(
        merge_dest.reshape(lane_count, 1, own_rows),
        segment_ids.reshape(lane_count, 1, own_rows),
        lengths, owners, residual_in, norm2_gain, norm2_bias, up_weight, up_bias,
        down_weight, down_bias, proj_weight, norm3_gain, norm3_bias, own_columns, gather,
    )


def solution(mesh):
    return jax.shard_map(
        body,
        mesh=mesh,
        in_specs=(
            P("req", None),
            P(("req", "mlp")),
            P(("req", "mlp")),
            P("req"),
            P("req"),
            P(),
            P(),
            P("mlp", None),
            P("mlp"),
            P("mlp", None),
            P(),
            P("mlp", None),
            P(),
            P(),
            P("req", None, None),
        ),
        out_specs=(P(("req", "mlp"), None), P(("req", "mlp"), None)),
        check_vma=False,
    )
```

```python
import functools
import math

import jax
import jax.numpy as jnp
from jax import lax
from jax.experimental import pallas as pl
from jax.experimental.pallas import tpu as pltpu
from jax.sharding import PartitionSpec as P

HEAD_DIM = 104
TAG_PAD = 128
EPSILON = 1e-06


VMEM_BYTES = 56 * 2**20
MESH = pl.DeviceIdType.MESH


def front_kernel(
    sizes,
    gather,
    places_ref,
    marks_ref,
    len_ref,
    owner_ref,
    up_bias_ref,
    params_ref,
    residual_hbm,
    up_hbm,
    down_hbm,
    proj_hbm,
    next_hbm,
    merged_ref,
    next_mixed_ref,
    mixed_ref,
    everyone_ref,
    next_ref,
    mix_ref,
    residual_ref,
    up_ref,
    down_ref,
    proj_ref,
    xq_ref,
    hidden_ref,
    acc_ref,
    core_out_ref,
    core_in_ref,
    y_out_ref,
    y_in_ref,
    share_ref,
    share_out_ref,
    share_in_ref,
    out_ref,
    in_ref,
    load_sem,
    core_send,
    core_recv,
    y_send,
    y_recv,
    share_send,
    share_recv,
    req_send,
    req_recv,
    all_send,
    all_recv,
    next_send,
    next_recv,
    mix_send,
    mix_recv,
):
    senders, slots, pad = sizes
    lanes = 4
    m = lax.axis_index("mlp")
    r = lax.axis_index("req")
    core_peer = m + 1 - 2 * (m % 2)
    y_peer = (m + 2) % lanes
    own_rows = places_ref.shape[-1]
    merged = own_rows // 4
    width = residual_ref.shape[1]
    wide = out_ref.shape[1]
    shard_rows = next_hbm.shape[0]
    heights = senders // 2
    x_peer = r + 1 - 2 * (r % 2)

    def shard(index):
        return pl.ds(pl.multiple_of(index * shard_rows, 16), shard_rows)

    z = r // 2

    def next_copy(source, send_slot, recv_slot, peer):
        rows = shard(source * 2 + r % 2)
        return pltpu.make_async_remote_copy(
            src_ref=next_ref.at[rows], dst_ref=next_ref.at[rows],
            send_sem=next_send.at[send_slot], recv_sem=next_recv.at[recv_slot],
            device_id={"req": peer}, device_id_type=MESH,
        )

    def up(source):
        return next_copy(source, source, source, (r + 2) % senders)

    def down(source):
        return next_copy(source, heights + source, source, (r + senders - 2) % senders)

    def across(source):
        return next_copy(source, 2 * heights + source, heights + source, x_peer)

    def spread_up(source):
        @pl.when(z < heights - 1)
        def _():
            up(source).start()

    def spread_down(source):
        @pl.when(z > 0)
        def _():
            down(source).start()

    def pass_on(d):
        if not gather:
            return

        @pl.when(z >= d)
        def _():
            up(z - d).wait_recv()
            spread_up(z - d)
            across(z - d).start()

        @pl.when(z + d < heights)
        def _():
            down(z + d).wait_recv()
            spread_down(z + d)
            across(z + d).start()

    loads = [
        pltpu.make_async_copy(a, b, load_sem.at[i])
        for i, (a, b) in enumerate(
            (
                (residual_hbm, residual_ref), (up_hbm, up_ref), (down_hbm, down_ref), (proj_hbm, proj_ref),
                (next_hbm, next_ref.at[shard(r)] if gather else next_ref),
            )
        )
    ]
    for load in loads:
        load.start()

    barrier = pltpu.get_barrier_semaphore()
    for k in range(1, lanes):
        pl.semaphore_signal(barrier, inc=1, device_id={"mlp": (m + k) % lanes}, device_id_type=MESH)

    def greet(k, c):
        pl.semaphore_signal(barrier, inc=1, device_id={"req": (r + k) % senders}, device_id_type=MESH)
        return c

    lax.fori_loop(1, senders, greet, 0)
    pl.semaphore_wait(barrier, lanes - 1 + senders - 1)

    def norm(values, gain, bias):
        mean_value = jnp.mean(values, axis=-1, keepdims=True)
        centred = values - mean_value
        spread = jnp.mean(centred * centred, axis=-1, keepdims=True)
        return centred * lax.rsqrt(spread + EPSILON) * gain + bias

    def core_copy(i):
        return pltpu.make_async_remote_copy(
            src_ref=core_out_ref.at[i], dst_ref=core_in_ref.at[i],
            send_sem=core_send.at[i], recv_sem=core_recv.at[i],
            device_id={"mlp": core_peer}, device_id_type=MESH,
        )

    y_copy = pltpu.make_async_remote_copy(
        src_ref=y_out_ref, dst_ref=y_in_ref, send_sem=y_send, recv_sem=y_recv,
        device_id={"mlp": y_peer}, device_id_type=MESH,
    )

    if gather:
        loads[4].wait()
        spread_up(z)
        spread_down(z)
        across(z).start()

    loads[0].wait()

    def quadrant_step(step, c):
        @pl.when(step == 2)
        def _():
            pass_on(1)

        first = 1 - step // 2
        second = 1 - step % 2
        q = (1 - second) * m + second * core_peer
        q = (1 - first) * q + first * ((q + 2) % lanes)
        want = 4 * lax.broadcasted_iota(jnp.int32, (merged, own_rows), 0) + q
        for b in range(lanes):
            hits = (want == places_ref[b]).astype(jnp.float32).astype(jnp.bfloat16)
            xq_ref[b * merged : (b + 1) * merged, :] = jnp.dot(
                hits,
                residual_ref[b * own_rows : (b + 1) * own_rows, :],
                preferred_element_type=jnp.float32,
            )
        normed = norm(xq_ref[...], params_ref[0:1, :], params_ref[1:2, :]).astype(jnp.bfloat16)

        @pl.when(step == 0)
        def _():
            loads[1].wait()

        hidden_total = up_ref.shape[0]
        for j in range(0, hidden_total, 256):
            upward = lax.dot_general(
                normed, up_ref[j : j + 256, :], (((1,), (1,)), ((), ())),
                preferred_element_type=jnp.float32,
            ) + up_bias_ref[:, j : j + 256]
            hidden_ref[:, j : j + 256] = (
                0.5 * upward * (1.0 + lax.erf(upward * math.sqrt(0.5)))
            ).astype(jnp.bfloat16)

        @pl.when(step == 0)
        def _():
            loads[2].wait()

        acc_ref[...] = jnp.dot(hidden_ref[...], down_ref[...], preferred_element_type=jnp.float32)

        @pl.when(step == 0)
        def _():
            core_out_ref[0] = acc_ref[...].astype(jnp.bfloat16)
            core_copy(0).start()

        @pl.when(step == 1)
        def _():
            core_copy(0).wait_recv()
            y_out_ref[...] = (acc_ref[...] + core_in_ref[0].astype(jnp.float32)).astype(jnp.bfloat16)
            y_copy.start()

        @pl.when(step == 2)
        def _():
            core_out_ref[1] = acc_ref[...].astype(jnp.bfloat16)
            core_copy(1).start()

        return c

    lax.fori_loop(0, lanes, quadrant_step, 0)
    pass_on(2)
    counts_row = len_ref[...] // 4
    down_index = lax.broadcasted_iota(jnp.int32, (senders, senders), 0)
    across_index = lax.broadcasted_iota(jnp.int32, (senders, senders), 1)
    counts_col = jnp.sum(
        jnp.where(across_index == down_index, counts_row, 0), axis=1, keepdims=True
    )
    owners_col = jnp.sum(
        jnp.where(across_index == down_index, owner_ref[...], 0), axis=1, keepdims=True
    )
    before = across_index < down_index
    starts = jnp.sum(jnp.where(before, counts_row, 0), axis=1, keepdims=True)
    index = lax.broadcasted_iota(jnp.int32, (senders, merged), 1)
    inside = (index >= starts) & (index < starts + counts_col)
    owner_of = jnp.sum(jnp.where(inside, owners_col, 0), axis=0, keepdims=True)
    begun = jnp.sum(jnp.where(inside, starts, 0), axis=0, keepdims=True)
    target = owner_of * pad + index[0:1, :] - begun
    route = (
        lax.broadcasted_iota(jnp.int32, (senders * pad, merged), 0) == target
    ).astype(jnp.float32).astype(jnp.bfloat16)
    first_hits = 4 * lax.broadcasted_iota(jnp.int32, (merged, own_rows), 0) == places_ref[m]
    row_tag = 1 + jnp.sum(jnp.where(first_hits, marks_ref[m], 0), axis=1, keepdims=True)
    tag_columns = jnp.broadcast_to(row_tag.astype(jnp.float32), (merged, wide - width))

    core_copy(1).wait_recv()
    y_copy.wait_recv()
    layer_out = (
        xq_ref[...] + (acc_ref[...] + core_in_ref[1].astype(jnp.float32) + y_in_ref[...].astype(jnp.float32))
        + params_ref[2:3, :]
    ).astype(jnp.bfloat16)
    loads[3].wait()
    acc_ref[...] = jnp.dot(layer_out, proj_ref[...], preferred_element_type=jnp.float32)
    for b in range(lanes):
        share_ref[b] = acc_ref[b * merged : (b + 1) * merged, :].astype(jnp.bfloat16)
    far = lanes - 1 - m

    def share_copy(slot, source, peer):
        return pltpu.make_async_remote_copy(
            src_ref=source, dst_ref=share_in_ref.at[slot],
            send_sem=share_send.at[slot], recv_sem=share_recv.at[slot],
            device_id={"mlp": peer}, device_id_type=MESH,
        )

    share_y = share_copy(2, share_out_ref, y_peer)
    shares = [
        share_copy(0, share_ref.at[far], core_peer),
        share_copy(1, share_ref.at[core_peer], core_peer),
        share_y,
    ]
    shares[0].start()
    shares[1].start()
    shares[0].wait_recv()
    share_out_ref[...] = (
        share_ref[y_peer].astype(jnp.float32) + share_in_ref[0].astype(jnp.float32)
    ).astype(jnp.bfloat16)
    share_y.start()
    for k in range(3, heights):
        pass_on(k)
    shares[1].wait_recv()
    total = share_ref[m].astype(jnp.float32) + share_in_ref[1].astype(jnp.float32)
    share_y.wait_recv()
    total = total + share_in_ref[2].astype(jnp.float32)
    extended = jnp.concatenate([total, tag_columns], axis=1).astype(jnp.bfloat16)
    out_ref[...] = jnp.dot(route, extended, preferred_element_type=jnp.float32).astype(jnp.bfloat16)

    def req_copy(k):
        to = (r + k) % senders
        return pltpu.make_async_remote_copy(
            src_ref=out_ref.at[pl.ds(pl.multiple_of(to * pad, 16), pad)],
            dst_ref=in_ref.at[pl.ds(pl.multiple_of(r * pad, 16), pad)],
            send_sem=req_send.at[k - 1], recv_sem=req_recv.at[k - 1],
            device_id={"req": to}, device_id_type=MESH,
        )

    def start_req(k, c):
        req_copy(k).start()
        return c

    lax.fori_loop(1, senders, start_req, 0)
    own = pl.ds(pl.multiple_of(r * pad, 16), pad)
    in_ref[own, :] = out_ref[own, :]
    def wait_req(k, c):
        req_copy(k).wait_recv()
        return c

    lax.fori_loop(1, senders, wait_req, 0)
    arrived = in_ref[...]
    if pad != slots:
        row = lax.broadcasted_iota(jnp.int32, (senders * slots, senders * pad), 0)
        column = lax.broadcasted_iota(jnp.int32, (senders * slots, senders * pad), 1)
        pick = (row // slots * pad + row % slots == column).astype(jnp.float32).astype(jnp.bfloat16)
        arrived = jnp.dot(pick, arrived, preferred_element_type=jnp.float32).astype(jnp.bfloat16)
    received = arrived[:, :width]
    merged_ref[...] = received
    everyone_ref[m, :, width:] = arrived[:, width:]
    everyone_ref[m, :, :width] = norm(
        received.astype(jnp.float32), params_ref[3:4, :], params_ref[4:5, :]
    ).astype(jnp.bfloat16)

    def row_copy(slot, block, peer):
        return pltpu.make_async_remote_copy(
            src_ref=everyone_ref.at[block], dst_ref=everyone_ref.at[block],
            send_sem=all_send.at[slot], recv_sem=all_recv.at[slot],
            device_id={"mlp": peer}, device_id_type=MESH,
        )

    row_y = row_copy(0, m, y_peer)
    row_core = row_copy(1, m, core_peer)
    row_y.start()
    row_core.start()
    if gather:
        for source in range(heights):
            across(source).wait_recv()
    else:
        loads[4].wait()
    part = next_ref.shape[1] // 3
    score_scale = 1.0 / math.sqrt(HEAD_DIM)
    recv_rows = senders * slots
    itself = lax.broadcasted_iota(jnp.int32, (recv_rows, recv_rows), 0) == lax.broadcasted_iota(
        jnp.int32, (recv_rows, recv_rows), 1
    )
    row_far = row_copy(2, y_peer, core_peer)

    def block_of(step):
        first = step // 2
        second = step % 2
        block = (1 - second) * m + second * core_peer
        return (1 - first) * block + first * ((block + 2) % lanes)

    def mix_copy(step):
        return pltpu.make_async_remote_copy(
            src_ref=mix_ref.at[block_of(step)], dst_ref=mixed_ref.at[m],
            send_sem=mix_send.at[step - 1], recv_sem=mix_recv.at[step - 1],
            device_id={"mlp": block_of(step)}, device_id_type=MESH,
        )

    def attend(step, c):
        @pl.when(step == 1)
        def _():
            row_core.wait_recv()

        @pl.when(step == 2)
        def _():
            row_y.wait_recv()
            row_far.start()

        @pl.when(step == 3)
        def _():
            row_far.wait_recv()

        block = block_of(step)
        rows = everyone_ref[block]
        heads = jnp.dot(rows[:, :width], next_ref[...], preferred_element_type=jnp.float32)
        tags = rows[:, width : width + recv_rows].astype(jnp.float32)
        key_tags = tags.T
        allowed = ((tags == key_tags) & (key_tags > 0.5)) | itself
        live = tags[:, :1] > 0.5
        outs = []
        for h in range(part // HEAD_DIM):
            at = h * HEAD_DIM
            query, key, value = (
                heads[:, i * part + at : i * part + at + HEAD_DIM].astype(jnp.bfloat16) for i in range(3)
            )
            scores = lax.dot_general(
                query, key, (((1,), (1,)), ((), ())), preferred_element_type=jnp.float32
            ) * score_scale
            weights = jnp.where(allowed, jnp.exp(scores), 0.0)
            probs = (weights / jnp.sum(weights, axis=-1, keepdims=True)).astype(jnp.bfloat16)
            mixed = jnp.dot(probs, value, preferred_element_type=jnp.float32)
            outs.append(jnp.where(live, mixed, 0.0))
        mix_ref[block] = jnp.concatenate(outs, axis=1).astype(jnp.bfloat16)

        @pl.when(step > 0)
        def _():
            mix_copy(step).start()

        return c

    lax.fori_loop(0, lanes, attend, 0)
    mixed_ref[m] = mix_ref[m]
    for step in range(1, lanes):
        mix_copy(step).wait()
    next_mixed_ref[...] = jnp.concatenate(
        [mixed_ref[b].astype(jnp.float32) for b in range(lanes)], axis=1
    ).astype(jnp.bfloat16)
    for copy in (core_copy(0), core_copy(1), y_copy, *shares, row_y, row_core, row_far):
        copy.wait_send()

    def drain(k, c):
        req_copy(k).wait_send()
        return c

    lax.fori_loop(1, senders, drain, 0)
    if gather:
        for source in range(heights):
            across(source).wait_send()

            @pl.when((source <= z) & (z < heights - 1))
            def _():
                up(source).wait_send()

            @pl.when((source >= z) & (z > 0))
            def _():
                down(source).wait_send()


def front(places, marks, lengths, owners, residual_in, norm2_gain, norm2_bias, up_weight, up_bias,
          down_weight, down_bias, proj_weight, norm3_gain, norm3_bias, next_part, gather):
    lanes, _, own_rows = places.shape
    senders = lengths.shape[0]
    width = residual_in.shape[1]
    merged = own_rows // 4
    slots = 2 * merged // senders
    pad = -(-slots // 16) * 16
    recv_rows = senders * slots
    wide = width + TAG_PAD
    hidden_own = up_weight.shape[0]
    bf16, f32 = jnp.bfloat16, jnp.float32
    small = [
        places, marks, lengths.reshape(1, -1), owners.reshape(1, -1), up_bias.reshape(1, -1),
        jnp.stack([norm2_gain, norm2_bias, down_bias, norm3_gain, norm3_bias]),
    ]
    large = [residual_in, up_weight, down_weight, proj_weight, next_part]
    dma = pltpu.SemaphoreType.DMA
    flops = 2 * own_rows * lanes * width * hidden_own * 2 + 2 * own_rows * width * width
    return pl.pallas_call(
        functools.partial(front_kernel, (senders, slots, pad), gather),
        out_shape=(
            jax.ShapeDtypeStruct((recv_rows, width), bf16),
            jax.ShapeDtypeStruct((recv_rows, width), bf16),
        ),
        in_specs=[pl.BlockSpec(memory_space=pltpu.VMEM)] * len(small)
        + [pl.BlockSpec(memory_space=pl.ANY)] * len(large),
        out_specs=(pl.BlockSpec(memory_space=pltpu.VMEM),) * 2,
        scratch_shapes=[
            pltpu.VMEM((lanes, recv_rows, next_part.shape[1] // 3), bf16),
            pltpu.VMEM((lanes, recv_rows, wide), bf16),
            pltpu.VMEM((width, next_part.shape[1]), bf16),
            pltpu.VMEM((lanes, recv_rows, next_part.shape[1] // 3), bf16),
            pltpu.VMEM(residual_in.shape, bf16),
            pltpu.VMEM(up_weight.shape, bf16),
            pltpu.VMEM(down_weight.shape, bf16),
            pltpu.VMEM(proj_weight.shape, bf16),
            pltpu.VMEM((own_rows, width), f32),
            pltpu.VMEM((own_rows, hidden_own), bf16),
            pltpu.VMEM((own_rows, width), f32),
            pltpu.VMEM((2, own_rows, width), bf16),
            pltpu.VMEM((2, own_rows, width), bf16),
            pltpu.VMEM((own_rows, width), bf16),
            pltpu.VMEM((own_rows, width), bf16),
            pltpu.VMEM((lanes, merged, width), bf16),
            pltpu.VMEM((merged, width), bf16),
            pltpu.VMEM((lanes - 1, merged, width), bf16),
            pltpu.VMEM((senders * pad, wide), bf16),
            pltpu.VMEM((senders * pad, wide), bf16),
            dma((5,)),
            dma((2,)), dma((2,)), dma, dma,
            dma((lanes - 1,)), dma((lanes - 1,)),
            dma((senders - 1,)), dma((senders - 1,)),
            dma((3,)), dma((3,)),
            dma((3 * senders // 2,)), dma((senders,)),
            dma((lanes - 1,)), dma((lanes - 1,)),
        ],
        compiler_params=pltpu.CompilerParams(
            collective_id=0, has_side_effects=True, vmem_limit_bytes=VMEM_BYTES
        ),
        cost_estimate=pl.CostEstimate(flops=flops * 4, bytes_accessed=64 * 2**20, transcendentals=0),
        name="front",
    )(*small, *large)


def body(
    residual_in,
    lengths,
    owners,
    merge_dest,
    segment_ids,
    norm2_gain,
    norm2_bias,
    up_weight,
    up_bias,
    down_weight,
    down_bias,
    proj_weight,
    norm3_gain,
    norm3_bias,
    next_weight,
):
    group_rows, model_width = residual_in.shape
    lane_count = lax.axis_size("mlp")
    lane_index = lax.axis_index("mlp")
    own_rows = group_rows // lane_count
    part_width = model_width // lane_count
    own_columns = lax.dynamic_slice_in_dim(
        next_weight, lane_index * part_width, part_width, 2
    ).reshape(next_weight.shape[0], -1)
    gather = next_weight.shape[0] % 16 == 0
    if not gather:
        own_columns = lax.all_gather(own_columns, "req", axis=0, tiled=True)
    return front(
        merge_dest.reshape(lane_count, 1, own_rows),
        segment_ids.reshape(lane_count, 1, own_rows),
        lengths, owners, residual_in, norm2_gain, norm2_bias, up_weight, up_bias,
        down_weight, down_bias, proj_weight, norm3_gain, norm3_bias, own_columns, gather,
    )


def solution(mesh):
    return jax.shard_map(
        body,
        mesh=mesh,
        in_specs=(
            P("req", None),
            P(("req", "mlp")),
            P(("req", "mlp")),
            P("req"),
            P("req"),
            P(),
            P(),
            P("mlp", None),
            P("mlp"),
            P("mlp", None),
            P(),
            P("mlp", None),
            P(),
            P(),
            P("req", None, None),
        ),
        out_specs=(P(("req", "mlp"), None), P(("req", "mlp"), None)),
        check_vma=False,
    )
```

```python
import functools
import math

import jax
import jax.numpy as jnp
from jax import lax
from jax.experimental import pallas as pl
from jax.experimental.pallas import tpu as pltpu
from jax.sharding import PartitionSpec as P

HEAD_DIM = 104
TAG_PAD = 128
EPSILON = 1e-06


VMEM_BYTES = 56 * 2**20
MESH = pl.DeviceIdType.MESH


def front_kernel(
    sizes,
    gather,
    places_ref,
    marks_ref,
    len_ref,
    owner_ref,
    up_bias_ref,
    gain2_ref,
    bias2_ref,
    down_bias_ref,
    gain3_ref,
    bias3_ref,
    residual_hbm,
    up_hbm,
    down_hbm,
    proj_hbm,
    next_hbm,
    merged_ref,
    next_mixed_ref,
    mixed_ref,
    everyone_ref,
    next_ref,
    mix_ref,
    residual_ref,
    up_ref,
    down_ref,
    proj_ref,
    xq_ref,
    hidden_ref,
    acc_ref,
    core_out_ref,
    core_in_ref,
    y_out_ref,
    y_in_ref,
    share_ref,
    share_out_ref,
    share_in_ref,
    out_ref,
    in_ref,
    load_sem,
    core_send,
    core_recv,
    y_send,
    y_recv,
    share_send,
    share_recv,
    req_send,
    req_recv,
    all_send,
    all_recv,
    next_send,
    next_recv,
    mix_send,
    mix_recv,
):
    senders, slots, pad = sizes
    lanes = 4
    m = lax.axis_index("mlp")
    r = lax.axis_index("req")
    core_peer = m + 1 - 2 * (m % 2)
    y_peer = (m + 2) % lanes
    own_rows = places_ref.shape[-1]
    merged = own_rows // 4
    width = residual_ref.shape[1]
    wide = out_ref.shape[1]
    shard_rows = next_hbm.shape[0]
    heights = senders // 2
    x_peer = r + 1 - 2 * (r % 2)

    def shard(index):
        return pl.ds(pl.multiple_of(index * shard_rows, 16), shard_rows)

    z = r // 2

    def next_copy(source, send_slot, recv_slot, peer):
        rows = shard(source * 2 + r % 2)
        return pltpu.make_async_remote_copy(
            src_ref=next_ref.at[rows], dst_ref=next_ref.at[rows],
            send_sem=next_send.at[send_slot], recv_sem=next_recv.at[recv_slot],
            device_id={"req": peer}, device_id_type=MESH,
        )

    def up(source):
        return next_copy(source, source, source, (r + 2) % senders)

    def down(source):
        return next_copy(source, heights + source, source, (r + senders - 2) % senders)

    def across(source):
        return next_copy(source, 2 * heights + source, heights + source, x_peer)

    def spread_up(source):
        @pl.when(z < heights - 1)
        def _():
            up(source).start()

    def spread_down(source):
        @pl.when(z > 0)
        def _():
            down(source).start()

    def pass_on(d):
        if not gather:
            return

        @pl.when(z >= d)
        def _():
            up(z - d).wait_recv()
            spread_up(z - d)
            across(z - d).start()

        @pl.when(z + d < heights)
        def _():
            down(z + d).wait_recv()
            spread_down(z + d)
            across(z + d).start()

    loads = [
        pltpu.make_async_copy(a, b, load_sem.at[i])
        for i, (a, b) in enumerate(
            (
                (residual_hbm, residual_ref), (up_hbm, up_ref), (down_hbm, down_ref), (proj_hbm, proj_ref),
                (next_hbm, next_ref.at[shard(r)] if gather else next_ref),
            )
        )
    ]
    for load in loads:
        load.start()

    barrier = pltpu.get_barrier_semaphore()
    for k in range(1, lanes):
        pl.semaphore_signal(barrier, inc=1, device_id={"mlp": (m + k) % lanes}, device_id_type=MESH)

    def greet(k, c):
        pl.semaphore_signal(barrier, inc=1, device_id={"req": (r + k) % senders}, device_id_type=MESH)
        return c

    lax.fori_loop(1, senders, greet, 0)
    pl.semaphore_wait(barrier, lanes - 1 + senders - 1)

    def row_of(ref):
        return ref[...].reshape(1, width)

    def norm(values, gain, bias):
        mean_value = jnp.mean(values, axis=-1, keepdims=True)
        centred = values - mean_value
        spread = jnp.mean(centred * centred, axis=-1, keepdims=True)
        return centred * lax.rsqrt(spread + EPSILON) * gain + bias

    def core_copy(i):
        return pltpu.make_async_remote_copy(
            src_ref=core_out_ref.at[i], dst_ref=core_in_ref.at[i],
            send_sem=core_send.at[i], recv_sem=core_recv.at[i],
            device_id={"mlp": core_peer}, device_id_type=MESH,
        )

    y_copy = pltpu.make_async_remote_copy(
        src_ref=y_out_ref, dst_ref=y_in_ref, send_sem=y_send, recv_sem=y_recv,
        device_id={"mlp": y_peer}, device_id_type=MESH,
    )

    if gather:
        loads[4].wait()
        spread_up(z)
        spread_down(z)
        across(z).start()

    loads[0].wait()

    def quadrant_step(step, c):
        @pl.when(step == 2)
        def _():
            pass_on(1)

        first = 1 - step // 2
        second = 1 - step % 2
        q = (1 - second) * m + second * core_peer
        q = (1 - first) * q + first * ((q + 2) % lanes)
        want = 4 * lax.broadcasted_iota(jnp.int32, (merged, own_rows), 0) + q
        for b in range(lanes):
            hits = (want == places_ref[b]).astype(jnp.float32).astype(jnp.bfloat16)
            xq_ref[b * merged : (b + 1) * merged, :] = jnp.dot(
                hits,
                residual_ref[b * own_rows : (b + 1) * own_rows, :],
                preferred_element_type=jnp.float32,
            )
        normed = norm(xq_ref[...], row_of(gain2_ref), row_of(bias2_ref)).astype(jnp.bfloat16)

        @pl.when(step == 0)
        def _():
            loads[1].wait()

        hidden_total = up_ref.shape[0]
        for j in range(0, hidden_total, 256):
            upward = lax.dot_general(
                normed, up_ref[j : j + 256, :], (((1,), (1,)), ((), ())),
                preferred_element_type=jnp.float32,
            ) + up_bias_ref[:, j : j + 256]
            hidden_ref[:, j : j + 256] = (
                0.5 * upward * (1.0 + lax.erf(upward * math.sqrt(0.5)))
            ).astype(jnp.bfloat16)

        @pl.when(step == 0)
        def _():
            loads[2].wait()

        acc_ref[...] = jnp.dot(hidden_ref[...], down_ref[...], preferred_element_type=jnp.float32)

        @pl.when(step == 0)
        def _():
            core_out_ref[0] = acc_ref[...].astype(jnp.bfloat16)
            core_copy(0).start()

        @pl.when(step == 1)
        def _():
            core_copy(0).wait_recv()
            y_out_ref[...] = (acc_ref[...] + core_in_ref[0].astype(jnp.float32)).astype(jnp.bfloat16)
            y_copy.start()

        @pl.when(step == 2)
        def _():
            core_out_ref[1] = acc_ref[...].astype(jnp.bfloat16)
            core_copy(1).start()

        return c

    lax.fori_loop(0, lanes, quadrant_step, 0)
    pass_on(2)
    counts_row = len_ref[...] // 4
    down_index = lax.broadcasted_iota(jnp.int32, (senders, senders), 0)
    across_index = lax.broadcasted_iota(jnp.int32, (senders, senders), 1)
    counts_col = jnp.sum(
        jnp.where(across_index == down_index, counts_row, 0), axis=1, keepdims=True
    )
    owners_col = jnp.sum(
        jnp.where(across_index == down_index, owner_ref[...], 0), axis=1, keepdims=True
    )
    before = across_index < down_index
    starts = jnp.sum(jnp.where(before, counts_row, 0), axis=1, keepdims=True)
    index = lax.broadcasted_iota(jnp.int32, (senders, merged), 1)
    inside = (index >= starts) & (index < starts + counts_col)
    owner_of = jnp.sum(jnp.where(inside, owners_col, 0), axis=0, keepdims=True)
    begun = jnp.sum(jnp.where(inside, starts, 0), axis=0, keepdims=True)
    target = owner_of * pad + index[0:1, :] - begun
    route = (
        lax.broadcasted_iota(jnp.int32, (senders * pad, merged), 0) == target
    ).astype(jnp.float32).astype(jnp.bfloat16)
    first_hits = 4 * lax.broadcasted_iota(jnp.int32, (merged, own_rows), 0) == places_ref[m]
    row_tag = 1 + jnp.sum(jnp.where(first_hits, marks_ref[m], 0), axis=1, keepdims=True)
    tag_columns = jnp.broadcast_to(row_tag.astype(jnp.float32), (merged, wide - width))

    core_copy(1).wait_recv()
    y_copy.wait_recv()
    layer_out = (
        xq_ref[...] + (acc_ref[...] + core_in_ref[1].astype(jnp.float32) + y_in_ref[...].astype(jnp.float32))
        + row_of(down_bias_ref)
    ).astype(jnp.bfloat16)
    loads[3].wait()
    acc_ref[...] = jnp.dot(layer_out, proj_ref[...], preferred_element_type=jnp.float32)
    for b in range(lanes):
        share_ref[b] = acc_ref[b * merged : (b + 1) * merged, :].astype(jnp.bfloat16)
    far = lanes - 1 - m

    def share_copy(slot, source, peer):
        return pltpu.make_async_remote_copy(
            src_ref=source, dst_ref=share_in_ref.at[slot],
            send_sem=share_send.at[slot], recv_sem=share_recv.at[slot],
            device_id={"mlp": peer}, device_id_type=MESH,
        )

    share_y = share_copy(2, share_out_ref, y_peer)
    shares = [
        share_copy(0, share_ref.at[far], core_peer),
        share_copy(1, share_ref.at[core_peer], core_peer),
        share_y,
    ]
    shares[0].start()
    shares[1].start()
    shares[0].wait_recv()
    share_out_ref[...] = (
        share_ref[y_peer].astype(jnp.float32) + share_in_ref[0].astype(jnp.float32)
    ).astype(jnp.bfloat16)
    share_y.start()
    for k in range(3, heights):
        pass_on(k)
    shares[1].wait_recv()
    total = share_ref[m].astype(jnp.float32) + share_in_ref[1].astype(jnp.float32)
    share_y.wait_recv()
    total = total + share_in_ref[2].astype(jnp.float32)
    extended = jnp.concatenate([total, tag_columns], axis=1).astype(jnp.bfloat16)
    out_ref[...] = jnp.dot(route, extended, preferred_element_type=jnp.float32).astype(jnp.bfloat16)

    def req_copy(k):
        to = (r + k) % senders
        return pltpu.make_async_remote_copy(
            src_ref=out_ref.at[pl.ds(pl.multiple_of(to * pad, 16), pad)],
            dst_ref=in_ref.at[pl.ds(pl.multiple_of(r * pad, 16), pad)],
            send_sem=req_send.at[k - 1], recv_sem=req_recv.at[k - 1],
            device_id={"req": to}, device_id_type=MESH,
        )

    def start_req(k, c):
        req_copy(k).start()
        return c

    lax.fori_loop(1, senders, start_req, 0)
    own = pl.ds(pl.multiple_of(r * pad, 16), pad)
    in_ref[own, :] = out_ref[own, :]
    def wait_req(k, c):
        req_copy(k).wait_recv()
        return c

    lax.fori_loop(1, senders, wait_req, 0)
    arrived = in_ref[...]
    if pad != slots:
        row = lax.broadcasted_iota(jnp.int32, (senders * slots, senders * pad), 0)
        column = lax.broadcasted_iota(jnp.int32, (senders * slots, senders * pad), 1)
        pick = (row // slots * pad + row % slots == column).astype(jnp.float32).astype(jnp.bfloat16)
        arrived = jnp.dot(pick, arrived, preferred_element_type=jnp.float32).astype(jnp.bfloat16)
    received = arrived[:, :width]
    merged_ref[...] = received
    everyone_ref[m, :, width:] = arrived[:, width:]
    everyone_ref[m, :, :width] = norm(
        received.astype(jnp.float32), row_of(gain3_ref), row_of(bias3_ref)
    ).astype(jnp.bfloat16)

    def row_copy(slot, block, peer):
        return pltpu.make_async_remote_copy(
            src_ref=everyone_ref.at[block], dst_ref=everyone_ref.at[block],
            send_sem=all_send.at[slot], recv_sem=all_recv.at[slot],
            device_id={"mlp": peer}, device_id_type=MESH,
        )

    row_y = row_copy(0, m, y_peer)
    row_core = row_copy(1, m, core_peer)
    row_y.start()
    row_core.start()
    if gather:
        for source in range(heights):
            across(source).wait_recv()
    else:
        loads[4].wait()
    part = next_ref.shape[1] // 3
    score_scale = 1.0 / math.sqrt(HEAD_DIM)
    recv_rows = senders * slots
    itself = lax.broadcasted_iota(jnp.int32, (recv_rows, recv_rows), 0) == lax.broadcasted_iota(
        jnp.int32, (recv_rows, recv_rows), 1
    )
    row_far = row_copy(2, y_peer, core_peer)

    def block_of(step):
        first = step // 2
        second = step % 2
        block = (1 - second) * m + second * core_peer
        return (1 - first) * block + first * ((block + 2) % lanes)

    def mix_copy(step):
        return pltpu.make_async_remote_copy(
            src_ref=mix_ref.at[block_of(step)], dst_ref=mixed_ref.at[m],
            send_sem=mix_send.at[step - 1], recv_sem=mix_recv.at[step - 1],
            device_id={"mlp": block_of(step)}, device_id_type=MESH,
        )

    def attend(step, c):
        @pl.when(step == 1)
        def _():
            row_core.wait_recv()

        @pl.when(step == 2)
        def _():
            row_y.wait_recv()
            row_far.start()

        @pl.when(step == 3)
        def _():
            row_far.wait_recv()

        block = block_of(step)
        rows = everyone_ref[block]
        heads = jnp.dot(rows[:, :width], next_ref[...], preferred_element_type=jnp.float32)
        tags = rows[:, width : width + recv_rows].astype(jnp.float32)
        key_tags = tags.T
        allowed = ((tags == key_tags) & (key_tags > 0.5)) | itself
        live = tags[:, :1] > 0.5
        outs = []
        for h in range(part // HEAD_DIM):
            at = h * HEAD_DIM
            query, key, value = (
                heads[:, i * part + at : i * part + at + HEAD_DIM].astype(jnp.bfloat16) for i in range(3)
            )
            scores = lax.dot_general(
                query, key, (((1,), (1,)), ((), ())), preferred_element_type=jnp.float32
            ) * score_scale
            weights = jnp.where(allowed, jnp.exp(scores), 0.0)
            probs = (weights / jnp.sum(weights, axis=-1, keepdims=True)).astype(jnp.bfloat16)
            mixed = jnp.dot(probs, value, preferred_element_type=jnp.float32)
            outs.append(jnp.where(live, mixed, 0.0))
        mix_ref[block] = jnp.concatenate(outs, axis=1).astype(jnp.bfloat16)

        @pl.when(step > 0)
        def _():
            mix_copy(step).start()

        return c

    lax.fori_loop(0, lanes, attend, 0)
    mixed_ref[m] = mix_ref[m]
    for step in range(1, lanes):
        mix_copy(step).wait()
    next_mixed_ref[...] = jnp.concatenate(
        [mixed_ref[b].astype(jnp.float32) for b in range(lanes)], axis=1
    ).astype(jnp.bfloat16)
    for copy in (core_copy(0), core_copy(1), y_copy, *shares, row_y, row_core, row_far):
        copy.wait_send()

    def drain(k, c):
        req_copy(k).wait_send()
        return c

    lax.fori_loop(1, senders, drain, 0)
    if gather:
        for source in range(heights):
            across(source).wait_send()

            @pl.when((source <= z) & (z < heights - 1))
            def _():
                up(source).wait_send()

            @pl.when((source >= z) & (z > 0))
            def _():
                down(source).wait_send()


def front(places, marks, lengths, owners, residual_in, norm2_gain, norm2_bias, up_weight, up_bias,
          down_weight, down_bias, proj_weight, norm3_gain, norm3_bias, next_part, gather):
    lanes, _, own_rows = places.shape
    senders = lengths.shape[0]
    width = residual_in.shape[1]
    merged = own_rows // 4
    slots = 2 * merged // senders
    pad = -(-slots // 16) * 16
    recv_rows = senders * slots
    wide = width + TAG_PAD
    hidden_own = up_weight.shape[0]
    bf16, f32 = jnp.bfloat16, jnp.float32
    small = [
        places, marks, lengths.reshape(1, -1), owners.reshape(1, -1), up_bias.reshape(1, -1),
        norm2_gain, norm2_bias, down_bias, norm3_gain, norm3_bias,
    ]
    large = [residual_in, up_weight, down_weight, proj_weight, next_part]
    dma = pltpu.SemaphoreType.DMA
    flops = 2 * own_rows * lanes * width * hidden_own * 2 + 2 * own_rows * width * width
    return pl.pallas_call(
        functools.partial(front_kernel, (senders, slots, pad), gather),
        out_shape=(
            jax.ShapeDtypeStruct((recv_rows, width), bf16),
            jax.ShapeDtypeStruct((recv_rows, width), bf16),
        ),
        in_specs=[pl.BlockSpec(memory_space=pltpu.VMEM)] * len(small)
        + [pl.BlockSpec(memory_space=pl.ANY)] * len(large),
        out_specs=(pl.BlockSpec(memory_space=pltpu.VMEM),) * 2,
        scratch_shapes=[
            pltpu.VMEM((lanes, recv_rows, next_part.shape[1] // 3), bf16),
            pltpu.VMEM((lanes, recv_rows, wide), bf16),
            pltpu.VMEM((width, next_part.shape[1]), bf16),
            pltpu.VMEM((lanes, recv_rows, next_part.shape[1] // 3), bf16),
            pltpu.VMEM(residual_in.shape, bf16),
            pltpu.VMEM(up_weight.shape, bf16),
            pltpu.VMEM(down_weight.shape, bf16),
            pltpu.VMEM(proj_weight.shape, bf16),
            pltpu.VMEM((own_rows, width), f32),
            pltpu.VMEM((own_rows, hidden_own), bf16),
            pltpu.VMEM((own_rows, width), f32),
            pltpu.VMEM((2, own_rows, width), bf16),
            pltpu.VMEM((2, own_rows, width), bf16),
            pltpu.VMEM((own_rows, width), bf16),
            pltpu.VMEM((own_rows, width), bf16),
            pltpu.VMEM((lanes, merged, width), bf16),
            pltpu.VMEM((merged, width), bf16),
            pltpu.VMEM((lanes - 1, merged, width), bf16),
            pltpu.VMEM((senders * pad, wide), bf16),
            pltpu.VMEM((senders * pad, wide), bf16),
            dma((5,)),
            dma((2,)), dma((2,)), dma, dma,
            dma((lanes - 1,)), dma((lanes - 1,)),
            dma((senders - 1,)), dma((senders - 1,)),
            dma((3,)), dma((3,)),
            dma((3 * senders // 2,)), dma((senders,)),
            dma((lanes - 1,)), dma((lanes - 1,)),
        ],
        compiler_params=pltpu.CompilerParams(
            collective_id=0, has_side_effects=True, vmem_limit_bytes=VMEM_BYTES
        ),
        cost_estimate=pl.CostEstimate(flops=flops * 4, bytes_accessed=64 * 2**20, transcendentals=0),
        name="front",
    )(*small, *large)


def body(
    residual_in,
    lengths,
    owners,
    merge_dest,
    segment_ids,
    norm2_gain,
    norm2_bias,
    up_weight,
    up_bias,
    down_weight,
    down_bias,
    proj_weight,
    norm3_gain,
    norm3_bias,
    next_weight,
):
    group_rows, model_width = residual_in.shape
    lane_count = lax.axis_size("mlp")
    lane_index = lax.axis_index("mlp")
    own_rows = group_rows // lane_count
    part_width = model_width // lane_count
    own_columns = lax.dynamic_slice_in_dim(
        next_weight, lane_index * part_width, part_width, 2
    ).reshape(next_weight.shape[0], -1)
    gather = next_weight.shape[0] % 16 == 0
    if not gather:
        own_columns = lax.all_gather(own_columns, "req", axis=0, tiled=True)
    return front(
        merge_dest.reshape(lane_count, 1, own_rows),
        segment_ids.reshape(lane_count, 1, own_rows),
        lengths, owners, residual_in, norm2_gain, norm2_bias, up_weight, up_bias,
        down_weight, down_bias, proj_weight, norm3_gain, norm3_bias, own_columns, gather,
    )


def solution(mesh):
    return jax.shard_map(
        body,
        mesh=mesh,
        in_specs=(
            P("req", None),
            P(("req", "mlp")),
            P(("req", "mlp")),
            P("req"),
            P("req"),
            P(),
            P(),
            P("mlp", None),
            P("mlp"),
            P("mlp", None),
            P(),
            P("mlp", None),
            P(),
            P(),
            P("req", None, None),
        ),
        out_specs=(P(("req", "mlp"), None), P(("req", "mlp"), None)),
        check_vma=False,
    )
```
